128 devices in a mesh: tp: 8 (over y, x_lo), ep: 16 (over x_hi, z, core).
Axes of the slice: x: 4 (x_hi: 2, x_lo: 2; x = x_hi * 2 + x_lo), y: 4, z: 4, core: 2. Of those that a mesh axis runs over, the one named last changes fastest.
Arguments:
- hidden: bfloat16 [16384, 18432], P(('ep', 'tp')), may hold values from -6 to 6
- output_gradient: bfloat16 [16384, 4608], P(('ep', 'tp')), may hold values from -6 to 6
- specialist_pairs: int32 [16384, 2], P(('ep', 'tp')), may hold values from 0 to 127, all different within a row; in each aligned block of 128 rows (0 to 127, 128 to 255, ...) at most 3 rows name the same one
- chosen_router_logits: float32 [16384, 2], P(('ep', 'tp')), may hold values from -6 to 6
- lowering_maps: bfloat16 [128, 18432, 32], P(('ep', 'tp')), may hold values from -0.046875 to 0.046875
- raising_maps: bfloat16 [128, 32, 4608], P(('ep', 'tp')), may hold values from -1 to 1
- dispatcher_map: bfloat16 [4608, 128], replicated, may hold values from -0.09375 to 0.09375
- queries: bfloat16 [16384, 2048], P('ep', 'tp'), may hold values from -15 to 15
- keys: bfloat16 [16384, 1024], P('ep', 'tp'), may hold values from -15 to 15
- values: bfloat16 [16384, 1024], P('ep', 'tp'), may hold values from -6 to 6
- context_gradient: bfloat16 [16384, 2048], P('ep', 'tp'), may hold values from -6 to 6
- query_projection: bfloat16 [4608, 2048], P(None, 'tp'), may hold values from -0.09375 to 0.09375
- key_projection: bfloat16 [4608, 1024], P(None, 'tp'), may hold values from -0.09375 to 0.09375
- value_projection: bfloat16 [4608, 1024], P(None, 'tp'), may hold values from -0.09375 to 0.09375
- lengths: int32 [16, 8], P('ep'), may hold values from 1 to 512, 1024 in all within a row
Outputs:
- residual_input_gradient: bfloat16 [16384, 4608], P(('ep', 'tp'))
- gated_hidden_gradient: bfloat16 [16384, 18432], P(('ep', 'tp'))
- router_logit_gradient: float32 [16384, 2], P(('ep', 'tp'))
- down_factors_gradient: bfloat16 [128, 18432, 32], P(('ep', 'tp'))
- up_factors_gradient: bfloat16 [128, 32, 4608], P(('ep', 'tp'))
The draws below stay inside these ranges and needn't reach their ends.
Inputs may be any that keep to these rules, and one draw needn't show every extreme that they name: `specialist_pairs`: each row names two different experts. In each aligned block of 128 rows (the rows of one device) no expert is named by more than 3 rows, and in every draw some expert is named by exactly 3 rows of some block. `lengths`: each row sums to 1024 and its largest entry is exactly 512.
All inputs are finite; a program needn't handle non-finite values.
Results may differ from the reference program's by a relative error of at most 0.015.
Values may be sent and summed in bfloat16 or wider, within the bound.
No kernel may reach another device: no remote copies, remote signals or barrier semaphores. Data moves between devices by JAX's collectives and lax.ppermute only.
A program may use at most 320 MiB of HBM per device.

```python
import math
import jax
import jax.numpy as jnp
import numpy as np
from jax import lax

EMBEDDING_SIZE = 4608
HD = 128
HEADS = 16
KV_HEADS = 8
NEURONS_PER_MLP = 18432
SPECIALIST_DEPTH = 32
SEQS = 8
ITEMS_PER_SHARD = 128
SPECIALIST_COUNT = 128
ROUTE_QUOTA = 3
SEQUENCE_ITEMS = 16384
N_TP = 8
N_EP = 16


def level_of(stream_key, extent, cuts, least, largest):
    factor_of = 1.0
    for position, shards_of in cuts:
        draws = jax.random.uniform(jax.random.fold_in(jax.random.fold_in(stream_key, 6), position), (shards_of,), jnp.float32, least / len(cuts), largest / len(cuts))
        factor_of = factor_of * jnp.repeat(jnp.exp(draws), extent[position] // shards_of).reshape((-1,) + (1,) * (len(extent) - 1 - position))
    return factor_of


def split_up(amount, total, bound, slope):
    portions = [(1 << 20) // math.isqrt(grade ** slope) + 1 for grade in range(2, amount + 1)]
    surplus, given = total - bound - (amount - 1), [1] * (amount - 1)
    while surplus > 0:
        movable = [i for i in range(amount - 1) if given[i] < bound]
        whole, left = sum([portions[i] for i in movable]), surplus
        for i in movable:
            extra = min(bound - given[i], max(1, left * portions[i] // whole), surplus)
            given[i] = given[i] + extra
            surplus = surplus - extra
    return np.array([bound] + given)


def ragged(own_key, number_of, total, reach, slope):
    if number_of == 2:
        one = jax.random.randint(own_key, (), max(1, total - reach), min(reach, total - 1) + 1)
        return jnp.stack([one, total - one])
    sizes = jnp.asarray(split_up(number_of, total, reach, slope), jnp.int32)
    twos = (number_of - 1) // 2
    giver, sink = sizes[1:1 + 2 * twos:2], sizes[2:2 + 2 * twos:2]
    slack = jnp.minimum(giver - 1, reach - sink)
    passed = jax.random.randint(jax.random.fold_in(own_key, 1), (twos,), 0, 1 << 20) % (slack + 1)
    sizes = sizes.at[1:1 + 2 * twos:2].set(giver - passed).at[2:2 + 2 * twos:2].set(sink + passed)
    return sizes[jax.random.permutation(jax.random.fold_in(own_key, 2), number_of)]


def shared_out(key, own, number, rows, count, top, reach, lean):
    sequence = jax.random.permutation(key, count)
    crowded, common = load_shares(count, rows * top, reach, lean, True), load_shares(count, rows * top, reach, lean, False)
    places = jnp.arange(count)

    def named(tallies, rotation):
        used = int((tallies > 0).sum())
        fixed = max(1, used // 4)
        shifted = fixed + (places - fixed + rotation * (used - fixed)) % max(1, count - fixed)
        return jnp.zeros((count,), jnp.int32).at[sequence[jnp.where(places < fixed, places, shifted)]].set(jnp.asarray(tallies, jnp.int32))

    tallies = jnp.where(number % 4 == 0, named(crowded, number // 4), named(common, number - number // 4 - 1))
    mixed = jax.random.permutation(jax.random.fold_in(own, 3), count)
    source_of, receiver = mixed[0:count // 2 * 2:2], mixed[1:count // 2 * 2:2]
    slack = jnp.minimum(tallies[source_of] - 1, reach - tallies[receiver]) // 2
    slack = jnp.where((source_of == sequence[0]) | (receiver == sequence[0]) | (tallies[receiver] == 0), 0, jnp.maximum(slack, 0))
    shifted = jax.random.randint(jax.random.fold_in(own, 4), (count // 2,), 0, 1 << 20) % (slack + 1)
    tallies = tallies.at[source_of].add(-shifted).at[receiver].add(shifted)
    members = jnp.searchsorted(jnp.cumsum(tallies), jnp.arange(rows * top), side="right").astype(jnp.int32)
    table = members.reshape(top, rows).T
    table = table[jax.random.permutation(jax.random.fold_in(own, 1), rows)]
    rotation = jax.random.randint(jax.random.fold_in(own, 2), (rows, 1), 0, top)
    return jnp.take_along_axis(table, (jnp.arange(top)[None, :] + rotation) % top, axis=1)


def load_shares(number_of, total, reach, skew, full):
    weights = [(1 << 20) // math.isqrt(grade ** skew) + 1 for grade in range(1, number_of + 1)]
    largest = reach if full else min(reach, max(-(-total // number_of), total * weights[0] // sum(weights)))
    least = 1 if total - largest >= number_of - 1 else 0
    counts, surplus = [largest] + [least] * (number_of - 1), total - largest - least * (number_of - 1)
    while surplus > 0:
        candidates = [i for i in range(1, number_of) if counts[i] < largest] or [i for i in range(1, number_of) if counts[i] < reach]
        mass, budget = sum([weights[i] for i in candidates]), surplus
        for i in candidates:
            addition = min(reach - counts[i], max(1, budget * weights[i] // mass), surplus)
            counts[i] = counts[i] + addition
            surplus = surplus - addition
    return np.array(counts)


def bell_draw(own_key, shape, deviation, most, cuts=(), kind=jnp.bfloat16):
    drawn = jax.random.normal(own_key, shape, jnp.float32) * deviation
    if len(cuts) > 0:
        drawn = level_of(own_key, shape, cuts, -0.22, 0.18) * drawn
    return jnp.clip(drawn, min=-most, max=most).astype(kind)


def setup_inputs(seed: int = 0) -> dict:
    splits = jax.random.split(jax.random.key(seed), 16)
    hidden = bell_draw(splits[0], (SEQUENCE_ITEMS, NEURONS_PER_MLP), 1.0, 6.0, ((0, 128),))
    output_gradient = bell_draw(splits[1], (SEQUENCE_ITEMS, EMBEDDING_SIZE), 1.0, 6.0, ((0, 128),))
    specialist_pairs_keys = jax.random.split(jax.random.fold_in(splits[2], 1), SEQUENCE_ITEMS // ITEMS_PER_SHARD)
    specialist_pairs_turns = jax.random.permutation(jax.random.fold_in(splits[2], 3), SEQUENCE_ITEMS // ITEMS_PER_SHARD)
    specialist_pairs = jax.vmap(lambda own, number: shared_out(jax.random.fold_in(splits[2], 2), own, number, ITEMS_PER_SHARD, SPECIALIST_COUNT, 2, ROUTE_QUOTA, 2))(specialist_pairs_keys, specialist_pairs_turns).reshape((SEQUENCE_ITEMS, 2))
    chosen_router_logits = bell_draw(splits[3], (SEQUENCE_ITEMS, 2), 1.0, 6.0, ((0, 128),), jnp.float32)
    lowering_maps = bell_draw(splits[4], (SPECIALIST_COUNT, NEURONS_PER_MLP, SPECIALIST_DEPTH), NEURONS_PER_MLP ** -0.5, 0.046875, ((0, 128),))
    raising_maps = bell_draw(splits[5], (SPECIALIST_COUNT, SPECIALIST_DEPTH, EMBEDDING_SIZE), SPECIALIST_DEPTH ** -0.5, 1.0, ((0, 128),))
    dispatcher_map = bell_draw(splits[6], (EMBEDDING_SIZE, SPECIALIST_COUNT), EMBEDDING_SIZE ** -0.5, 0.09375)
    queries = bell_draw(splits[7], (SEQUENCE_ITEMS, HEADS * HD), 2.5, 15.0, ((0, 16), (1, 8)))
    keys = bell_draw(splits[8], (SEQUENCE_ITEMS, KV_HEADS * HD), 2.5, 15.0, ((0, 16), (1, 8)))
    values = bell_draw(splits[9], (SEQUENCE_ITEMS, KV_HEADS * HD), 1.0, 6.0, ((0, 16), (1, 8)))
    context_gradient = bell_draw(splits[10], (SEQUENCE_ITEMS, HEADS * HD), 1.0, 6.0, ((0, 16), (1, 8)))
    query_projection = bell_draw(splits[11], (EMBEDDING_SIZE, HEADS * HD), EMBEDDING_SIZE ** -0.5, 0.09375, ((1, 8),))
    key_projection = bell_draw(splits[12], (EMBEDDING_SIZE, KV_HEADS * HD), EMBEDDING_SIZE ** -0.5, 0.09375, ((1, 8),))
    value_projection = bell_draw(splits[13], (EMBEDDING_SIZE, KV_HEADS * HD), EMBEDDING_SIZE ** -0.5, 0.09375, ((1, 8),))
    lengths = jax.vmap(lambda own: ragged(own, SEQS, ITEMS_PER_SHARD * N_TP, ITEMS_PER_SHARD * N_TP // 2, 2))(jax.random.split(splits[14], N_EP)).reshape((N_EP, SEQS)).astype(jnp.int32)
    return dict(hidden=hidden, output_gradient=output_gradient, specialist_pairs=specialist_pairs, chosen_router_logits=chosen_router_logits, lowering_maps=lowering_maps, raising_maps=raising_maps, dispatcher_map=dispatcher_map, queries=queries, keys=keys, values=values, context_gradient=context_gradient, query_projection=query_projection, key_projection=key_projection, value_projection=value_projection, lengths=lengths)


adapter_scale = 2.0
score_cap = 50.0
query_scale = 144.0 ** -0.5


def attend_backward(queries, keys, values, context_gradient, lengths, query_projection, key_projection, value_projection):
    rows = queries.shape[0]
    kv_count = keys.shape[1] // HD
    group = queries.shape[1] // keys.shape[1]
    query4 = queries.reshape(rows, kv_count, group, HD)
    ctx4 = context_gradient.reshape(rows, kv_count, group, HD)
    key3 = keys.reshape(rows, kv_count, HD)
    value3 = values.reshape(rows, kv_count, HD)
    places = jnp.arange(rows, dtype=jnp.int32)
    bounds = jnp.cumsum(lengths.astype(jnp.int32))
    docs = jnp.sum((places[:, None] >= bounds[None, :]).astype(jnp.int32), axis=1)
    allowed = (docs[:, None] == docs[None, :]) & (places[:, None] >= places[None, :])
    raw = jnp.einsum("ikgd,jkd->kgij", query4.astype(jnp.float32), key3.astype(jnp.float32)) * query_scale
    bent = jnp.tanh(raw / score_cap)
    expo = jnp.where(allowed, jnp.exp(score_cap * bent), 0.0)
    probs = expo / jnp.sum(expo, axis=-1, keepdims=True)
    dprobs = jnp.einsum("ikgd,jkd->kgij", ctx4.astype(jnp.float32), value3.astype(jnp.float32))
    dsoft = probs * (dprobs - jnp.sum(probs * dprobs, axis=-1, keepdims=True))
    dscore = (dsoft * (1.0 - bent * bent)).astype(jnp.bfloat16).astype(jnp.float32)
    probs_b = probs.astype(jnp.bfloat16).astype(jnp.float32)
    dquery = (jnp.einsum("kgij,jkd->ikgd", dscore, key3.astype(jnp.float32)) * query_scale).astype(jnp.bfloat16).reshape(rows, -1)
    dkey = (jnp.einsum("kgij,ikgd->jkd", dscore, query4.astype(jnp.float32)) * query_scale).astype(jnp.bfloat16).reshape(rows, -1)
    dvalue = jnp.einsum("kgij,ikgd->jkd", probs_b, ctx4.astype(jnp.float32)).astype(jnp.bfloat16).reshape(rows, -1)
    part = jnp.einsum("te,de->td", dquery.astype(jnp.float32), query_projection.astype(jnp.float32))
    part = part + jnp.einsum("te,de->td", dkey.astype(jnp.float32), key_projection.astype(jnp.float32))
    part = part + jnp.einsum("te,de->td", dvalue.astype(jnp.float32), value_projection.astype(jnp.float32))
    return part


def single_expert_backward(rows_h, width_rows, rows_w, a_mat, up_factor_matrix):
    latent_value = jnp.dot(rows_h, a_mat, preferred_element_type=jnp.float32).astype(jnp.bfloat16)
    output_change = adapter_scale * jnp.dot(latent_value, up_factor_matrix, preferred_element_type=jnp.float32)
    gate_weight_value = jnp.sum(width_rows.astype(jnp.float32) * output_change, axis=-1).astype(jnp.bfloat16)
    expert_weight = rows_w.astype(jnp.float32)[:, None]
    projected_rows = jnp.einsum("sd,rd->sr", width_rows.astype(jnp.float32), up_factor_matrix.astype(jnp.float32))
    latent_gradient = (adapter_scale * expert_weight * projected_rows).astype(jnp.bfloat16)
    weighted_latent = (expert_weight * latent_value.astype(jnp.float32)).astype(jnp.bfloat16)
    up_factor_grad = (adapter_scale * jnp.einsum("km,kv->mv", weighted_latent.astype(jnp.float32), width_rows.astype(jnp.float32))).astype(jnp.bfloat16)
    down_factor_grad = jnp.einsum("sf,sr->fr", rows_h.astype(jnp.float32), latent_gradient.astype(jnp.float32)).astype(jnp.bfloat16)
    hidden_unit_grad = jnp.einsum("sr,fr->sf", latent_gradient.astype(jnp.float32), a_mat.astype(jnp.float32)).astype(jnp.bfloat16)
    return hidden_unit_grad, gate_weight_value, down_factor_grad, up_factor_grad


def router_term(specialist_pairs, weights, gates, dispatcher_map, experts):
    gate_val = gates.astype(jnp.float32)
    router_logit_gradient = weights * (gate_val - jnp.sum(weights * gate_val, axis=-1, keepdims=True))
    ids = jnp.arange(experts, dtype=jnp.int32)
    expert_table = jnp.sum(jnp.where(specialist_pairs[:, :, None] == ids[None, None, :], router_logit_gradient[:, :, None], 0.0), axis=1)
    expert_table = expert_table.astype(jnp.bfloat16)
    term = jnp.einsum("te,de->td", expert_table.astype(jnp.float32), dispatcher_map.astype(jnp.float32))
    return router_logit_gradient, term


def reference(hidden, output_gradient, specialist_pairs, chosen_router_logits, lowering_maps, raising_maps, dispatcher_map, queries, keys, values, context_gradient, query_projection, key_projection, value_projection, lengths):
    experts = N_TP * N_EP
    devices = N_TP * N_EP
    weights = jax.nn.softmax(chosen_router_logits, axis=-1)
    weights_b = weights.astype(jnp.bfloat16)
    flat = specialist_pairs.reshape(devices, 2 * ITEMS_PER_SHARD)
    hot = (flat[:, :, None] == jnp.arange(experts, dtype=jnp.int32)[None, None, :]).astype(jnp.int32)
    slot = jnp.sum(hot * (jnp.cumsum(hot, axis=1) - 1), axis=2)
    source = jnp.arange(devices, dtype=jnp.int32)[:, None]
    place = flat * (devices * ROUTE_QUOTA) + source * ROUTE_QUOTA + slot
    entries = jnp.arange(2 * SEQUENCE_ITEMS, dtype=jnp.int32)
    expert_table = jnp.full((experts * devices * ROUTE_QUOTA,), 2 * SEQUENCE_ITEMS, jnp.int32).at[place.reshape(-1)].set(entries)
    expert_table = expert_table.reshape(experts, devices * ROUTE_QUOTA)
    hidden_pad = jnp.concatenate([hidden, jnp.zeros((1, NEURONS_PER_MLP), hidden.dtype)], axis=0)
    grad_pad = jnp.concatenate([output_gradient, jnp.zeros((1, EMBEDDING_SIZE), output_gradient.dtype)], axis=0)
    weight_pad = jnp.concatenate([weights_b.reshape(-1), jnp.zeros((1,), jnp.bfloat16)], axis=0)

    def expert_results(carry, inputs):
        index, a_mat, up_factor_matrix = inputs
        token_index = index // 2
        hidden_unit_grad, gate_weight_value, down_factor_grad, up_factor_grad = single_expert_backward(hidden_pad[token_index], grad_pad[token_index], weight_pad[index], a_mat, up_factor_matrix)
        stored_hidden = carry[0].at[index].set(hidden_unit_grad)
        stored_gradient = carry[1].at[index].set(gate_weight_value)
        return (stored_hidden, stored_gradient), (down_factor_grad, up_factor_grad)

    start_offset = (jnp.zeros((2 * SEQUENCE_ITEMS + 1, NEURONS_PER_MLP), jnp.bfloat16), jnp.zeros((2 * SEQUENCE_ITEMS + 1,), jnp.bfloat16))
    (stored_hidden, stored_gradient), (down_factors_gradient, up_factors_gradient) = lax.scan(expert_results, start_offset, (expert_table, lowering_maps, raising_maps))
    gated_hidden_gradient = (stored_hidden[0:2 * SEQUENCE_ITEMS:2].astype(jnp.float32) + stored_hidden[1:2 * SEQUENCE_ITEMS:2].astype(jnp.float32)).astype(jnp.bfloat16)
    gates = stored_gradient[:2 * SEQUENCE_ITEMS].reshape(SEQUENCE_ITEMS, 2)
    router_logit_gradient, term = router_term(specialist_pairs, weights, gates, dispatcher_map, experts)

    group_rows = ITEMS_PER_SHARD * N_TP
    q_cols = HEADS * HD // N_TP
    k_cols = KV_HEADS * HD // N_TP

    def per_group(group_index):
        row0 = (group_index * group_rows).astype(jnp.int32)
        q_rows = lax.dynamic_slice_in_dim(queries, row0, group_rows, 0)
        k_rows = lax.dynamic_slice_in_dim(keys, row0, group_rows, 0)
        v_rows = lax.dynamic_slice_in_dim(values, row0, group_rows, 0)
        c_rows = lax.dynamic_slice_in_dim(context_gradient, row0, group_rows, 0)
        doc_lengths = lengths[group_index]

        def per_heads(carry, head_group):
            qc = (head_group * q_cols).astype(jnp.int32)
            kc = (head_group * k_cols).astype(jnp.int32)
            part = attend_backward(
                lax.dynamic_slice_in_dim(q_rows, qc, q_cols, 1),
                lax.dynamic_slice_in_dim(k_rows, kc, k_cols, 1),
                lax.dynamic_slice_in_dim(v_rows, kc, k_cols, 1),
                lax.dynamic_slice_in_dim(c_rows, qc, q_cols, 1),
                doc_lengths,
                lax.dynamic_slice_in_dim(query_projection, qc, q_cols, 1),
                lax.dynamic_slice_in_dim(key_projection, kc, k_cols, 1),
                lax.dynamic_slice_in_dim(value_projection, kc, k_cols, 1))
            return carry + part.astype(jnp.bfloat16).astype(jnp.float32), None

        total, unused = lax.scan(per_heads, jnp.zeros((group_rows, EMBEDDING_SIZE), jnp.float32), jnp.arange(N_TP, dtype=jnp.int32))
        return total

    attention_term = lax.map(per_group, jnp.arange(N_EP, dtype=jnp.int32)).reshape(SEQUENCE_ITEMS, EMBEDDING_SIZE)
    residual_input_gradient = (output_gradient.astype(jnp.float32) + term + attention_term).astype(jnp.bfloat16)
    return (residual_input_gradient, gated_hidden_gradient, router_logit_gradient, down_factors_gradient, up_factors_gradient)
```

```python
import jax
import jax.numpy as jnp
from jax import lax
from jax.experimental import pallas as pl
from jax.experimental.pallas import tpu as pltpu
from jax.sharding import Mesh, PartitionSpec as P

HD = 128
RANK = 32
PLANE = ("xl", "xh", "z", "c")
LINE = "y"
TP = ("y", "xl")
EP = ("xh", "z", "c")
ROWS = ("xh", "z", "c", "y", "xl")

SLICES = 32
WIDTH = 768
HWIDE = 640

adapter_scale = 2.0
score_cap = 50.0
query_scale = 144.0 ** (-0.5)
F32 = jnp.float32
BF16 = jnp.bfloat16
VMEM = 60 * 1024 * 1024


def attend_backward(
    queries,
    keys,
    values,
    context_gradient,
    lengths,
    query_projection,
    key_projection,
    value_projection,
):
    rows = queries.shape[0]
    kv_count = keys.shape[1] // HD
    group = queries.shape[1] // keys.shape[1]
    query4 = queries.reshape(rows, kv_count, group, HD)
    ctx4 = context_gradient.reshape(rows, kv_count, group, HD)
    key3 = keys.reshape(rows, kv_count, HD)
    value3 = values.reshape(rows, kv_count, HD)
    places = jnp.arange(rows, dtype=jnp.int32)
    bounds = jnp.cumsum(lengths)
    docs = jnp.sum((places[:, None] >= bounds[None, :]).astype(jnp.int32), axis=1)
    allowed = (docs[:, None] == docs[None, :]) & (places[:, None] >= places[None, :])
    raw = (
        jnp.einsum("ikgd,jkd->kgij", query4, key3, preferred_element_type=jnp.float32) * query_scale
    )
    bent = jnp.tanh(raw / score_cap)
    expo = jnp.where(allowed, jnp.exp(score_cap * bent), 0.0)
    probs = expo / jnp.sum(expo, axis=-1, keepdims=True)
    dprobs = jnp.einsum("ikgd,jkd->kgij", ctx4, value3, preferred_element_type=jnp.float32)
    dsoft = probs * (dprobs - jnp.sum(probs * dprobs, axis=-1, keepdims=True))
    dscore = (dsoft * (1.0 - bent * bent)).astype(jnp.bfloat16)
    probs_b = probs.astype(jnp.bfloat16)
    dquery = (
        (
            jnp.einsum("kgij,jkd->ikgd", dscore, key3, preferred_element_type=jnp.float32)
            * query_scale
        )
        .astype(jnp.bfloat16)
        .reshape(rows, -1)
    )
    dkey = (
        (
            jnp.einsum("kgij,ikgd->jkd", dscore, query4, preferred_element_type=jnp.float32)
            * query_scale
        )
        .astype(jnp.bfloat16)
        .reshape(rows, -1)
    )
    dvalue = (
        jnp.einsum("kgij,ikgd->jkd", probs_b, ctx4, preferred_element_type=jnp.float32)
        .astype(jnp.bfloat16)
        .reshape(rows, -1)
    )
    grads = jnp.concatenate([dquery, dkey, dvalue], axis=1)
    maps = jnp.concatenate([query_projection, key_projection, value_projection], axis=1)
    return jnp.einsum("te,de->td", grads, maps, preferred_element_type=jnp.float32)


def lanes_of(shape):
    return lax.broadcasted_iota(jnp.int32, shape, len(shape) - 1)


def pack_kernel(hm_ref, hr_ref, gm_ref, gr_ref, id_ref, out_ref):
    rows = hm_ref.shape[0]
    lane = lanes_of((rows, 128))
    ids = id_ref[...]
    extra = gr_ref[...].astype(F32)
    extra = jnp.where(pl.program_id(0) % 2 == 0, extra, pltpu.roll(extra, 64, 1))
    for q in range(4):
        out_ref[q, :, 0:512] = hm_ref[:, 512 * q : 512 * q + 512]
        hid = hr_ref[:, 128 * (q // 2) : 128 * (q // 2) + 128].astype(F32)
        if q % 2:
            hid = pltpu.roll(hid, 64, 1)
        grad = pltpu.roll(extra, 64 - 16 * q, 1)
        tail = jnp.where(lane < 64, hid, jnp.where(lane < 80, grad, ids))
        out_ref[q, :, 512:640] = tail.astype(BF16)
        out_ref[q, :, 640:768] = gm_ref[:, 128 * q : 128 * q + 128]


def pack(hid, grad, ids):
    rows = hid.shape[0]
    return pl.pallas_call(
        pack_kernel,
        grid=(8,),
        in_specs=[
            pl.BlockSpec((rows, 2048), lambda i: (0, i)),
            pl.BlockSpec((rows, 256), lambda i: (0, 64 + i)),
            pl.BlockSpec((rows, 512), lambda i: (0, i)),
            pl.BlockSpec((rows, 128), lambda i: (0, 32 + i // 2)),
            pl.BlockSpec((rows, 128), lambda i: (0, 0)),
        ],
        out_specs=pl.BlockSpec((4, rows, WIDTH), lambda i: (i, 0, 0)),
        out_shape=jax.ShapeDtypeStruct((SLICES, rows, WIDTH), BF16),
        compiler_params=pltpu.CompilerParams(vmem_limit_bytes=VMEM),
        cost_estimate=pl.CostEstimate(
            flops=rows * 2 * 24576, bytes_accessed=rows * 2 * 49152, transcendentals=0
        ),
        name="pack_slices",
    )(hid, hid, grad, grad, ids)


def unpack_kernel(main_ref, rem_ref, out_ref):
    @pl.when(pl.program_id(0) < 8)
    def _():
        for q in range(4):
            out_ref[:, 512 * q : 512 * q + 512] = main_ref[q]

    @pl.when(pl.program_id(0) == 8)
    def _():
        lane = lanes_of(rem_ref.shape[1:])
        for d in range(16):
            low = rem_ref[2 * d].astype(F32)
            high = pltpu.roll(rem_ref[2 * d + 1].astype(F32), 64, 1)
            out_ref[:, 128 * d : 128 * d + 128] = jnp.where(lane < 64, low, high).astype(BF16)


def unpack(blocks):
    rows = blocks.shape[1]
    return pl.pallas_call(
        unpack_kernel,
        grid=(9,),
        in_specs=[
            pl.BlockSpec((4, rows, 512), lambda i: (jnp.minimum(i, 7), 0, 0)),
            pl.BlockSpec((SLICES, rows, 128), lambda i: (0, 0, 4)),
        ],
        out_specs=pl.BlockSpec((rows, 2048), lambda i: (0, i)),
        out_shape=jax.ShapeDtypeStruct((rows, 18432), BF16),
        compiler_params=pltpu.CompilerParams(vmem_limit_bytes=VMEM),
        cost_estimate=pl.CostEstimate(
            flops=rows * 18432, bytes_accessed=rows * 4 * 19000, transcendentals=0
        ),
        name="unpack_slices",
    )(blocks, blocks)


def fold_matrix(k):
    r = lax.broadcasted_iota(jnp.int32, (128, 128), 0)
    c = lax.broadcasted_iota(jnp.int32, (128, 128), 1)
    return (c == r % RANK + RANK * k).astype(F32).astype(BF16)


def spread_matrix(k):
    r = lax.broadcasted_iota(jnp.int32, (128, 128), 0)
    c = lax.broadcasted_iota(jnp.int32, (128, 128), 1)
    return (r == c % RANK + RANK * k).astype(F32).astype(BF16)


def contract_kernel(x_ref, w_ref, id_ref, out_ref, h_ref, g_ref, a0, a1, b0, b1):
    rows = x_ref.shape[0]
    step = 512
    lane = lanes_of((rows, 128))
    tail = x_ref[:, 512:640]
    zero = jnp.zeros_like(tail)
    h_ref[:, 0:512] = x_ref[:, 0:512]
    h_ref[:, 512:640] = jnp.where(lane < 64, tail, zero)
    g_ref[:, 0:128] = jnp.where((lane >= 64) & (lane < 80), tail, zero)
    g_ref[:, 128:256] = x_ref[:, 640:768]
    for acc in (a0, a1, b0, b1):
        acc[...] = jnp.zeros_like(acc)
    e0 = id_ref[:, 0:1] - lane // RANK
    e1 = id_ref[:, 1:2] - lane // RANK
    dims = (((1,), (1,)), ((), ()))

    def body(n, carry):
        start = pl.multiple_of(n * step, step)
        w_h = w_ref[pl.ds(start, step), 0:640]
        w_g = w_ref[pl.ds(start, step), 512:768]
        z = lax.dot_general(h_ref[...], w_h, dims, preferred_element_type=F32)
        p = lax.dot_general(g_ref[...], w_g, dims, preferred_element_type=F32)
        for refs, part in (((a0, a1), z), ((b0, b1), p)):
            for ref, e in zip(refs, (e0, e1)):
                acc = ref[...]
                for j in range(step // 128):
                    here = e == n * (step // RANK) + 4 * j
                    acc = jnp.where(here, part[:, 128 * j : 128 * j + 128], acc)
                ref[...] = acc
        return carry

    lax.fori_loop(0, w_ref.shape[0] // step, body, 0)
    out = jnp.zeros((rows, 128), F32)
    for k, acc in enumerate((a0, b0, a1, b1)):
        out += jnp.dot(acc[...].astype(BF16), fold_matrix(k), preferred_element_type=F32)
    out_ref[...] = out.astype(BF16)


def contract(x, w, ids):
    rows, tile = x.shape[0], 512
    return pl.pallas_call(
        contract_kernel,
        grid=(rows // tile,),
        in_specs=[
            pl.BlockSpec((tile, WIDTH), lambda i: (i, 0)),
            pl.BlockSpec(w.shape, lambda i: (0, 0)),
            pl.BlockSpec((tile, 2), lambda i: (i, 0)),
        ],
        out_specs=pl.BlockSpec((tile, 128), lambda i: (i, 0)),
        out_shape=jax.ShapeDtypeStruct((rows, 128), BF16),
        scratch_shapes=[pltpu.VMEM((tile, HWIDE), BF16), pltpu.VMEM((tile, 256), BF16)]
        + [pltpu.VMEM((tile, 128), F32)] * 4,
        compiler_params=pltpu.CompilerParams(vmem_limit_bytes=VMEM),
        cost_estimate=pl.CostEstimate(
            flops=2 * rows * w.shape[0] * 1024,
            bytes_accessed=2 * (rows + w.shape[0]) * WIDTH,
            transcendentals=0,
        ),
        name="contract_experts",
    )(x, w, ids)


def factors_kernel(x_ref, dt_ref, it_ref, out_ref, acc_h, acc_g):
    tile, total = out_ref.shape[0], x_ref.shape[0]
    step = 1024
    acc_h[...] = jnp.zeros_like(acc_h)
    acc_g[...] = jnp.zeros_like(acc_g)
    first = pl.program_id(0) * (tile // RANK)

    def body(n, carry):
        start = pl.multiple_of(n * step, step)
        at = pl.ds(start, step)
        e0, e1 = it_ref[0:1, at], it_ref[1:2, at]
        d0, w0 = dt_ref[0:32, at], dt_ref[32:64, at]
        d1, w1 = dt_ref[64:96, at], dt_ref[96:128, at]
        d_parts, w_parts = [], []
        for j in range(tile // RANK):
            m0, m1 = e0 == first + j, e1 == first + j
            d_parts.append(jnp.where(m0, d0, jnp.where(m1, d1, 0.0)).astype(BF16))
            w_parts.append(jnp.where(m0, w0, jnp.where(m1, w1, 0.0)).astype(BF16))
        d_all = jnp.concatenate(d_parts, axis=0)
        w_all = jnp.concatenate(w_parts, axis=0)
        acc_h[...] += jnp.dot(d_all, x_ref[at, 0:640], preferred_element_type=F32)
        acc_g[...] += jnp.dot(w_all, x_ref[at, 512:768], preferred_element_type=F32)
        return carry

    lax.fori_loop(0, total // step, body, 0)
    lane = lanes_of((tile, 128))
    out_ref[:, 0:512] = acc_h[:, 0:512].astype(BF16)
    out_ref[:, 512:640] = jnp.where(lane < 64, acc_h[:, 512:640], acc_g[:, 0:128]).astype(BF16)
    out_ref[:, 640:768] = acc_g[:, 128:256].astype(BF16)


def factors(x, dt, it, columns):
    tile = 512
    return pl.pallas_call(
        factors_kernel,
        grid=(columns // tile,),
        in_specs=[
            pl.BlockSpec(x.shape, lambda i: (0, 0)),
            pl.BlockSpec(dt.shape, lambda i: (0, 0)),
            pl.BlockSpec(it.shape, lambda i: (0, 0)),
        ],
        out_specs=pl.BlockSpec((tile, WIDTH), lambda i: (i, 0)),
        out_shape=jax.ShapeDtypeStruct((columns, WIDTH), BF16),
        scratch_shapes=[pltpu.VMEM((tile, HWIDE), F32), pltpu.VMEM((tile, 256), F32)],
        compiler_params=pltpu.CompilerParams(vmem_limit_bytes=VMEM),
        cost_estimate=pl.CostEstimate(
            flops=2 * x.shape[0] * columns * 1024,
            bytes_accessed=2 * (x.shape[0] + columns) * WIDTH,
            transcendentals=0,
        ),
        name="factor_gradients",
    )(x, dt, it)


def expand_kernel(d_ref, w_ref, id_ref, out_ref, acc):
    rows = d_ref.shape[0]
    step = 512
    lane = lanes_of((rows, 128))
    e0 = id_ref[:, 0:1] - lane // RANK
    e1 = id_ref[:, 1:2] - lane // RANK
    d0 = jnp.dot(d_ref[...], spread_matrix(0), preferred_element_type=F32)
    d1 = jnp.dot(d_ref[...], spread_matrix(2), preferred_element_type=F32)
    acc[...] = jnp.zeros_like(acc)

    def body(n, carry):
        start = pl.multiple_of(n * step, step)
        parts = []
        for j in range(step // 128):
            at = n * (step // RANK) + 4 * j
            parts.append(jnp.where(e0 == at, d0, jnp.where(e1 == at, d1, 0.0)).astype(BF16))
        spread = jnp.concatenate(parts, axis=1)
        acc[...] += jnp.dot(spread, w_ref[pl.ds(start, step), 0:640], preferred_element_type=F32)
        return carry

    lax.fori_loop(0, w_ref.shape[0] // step, body, 0)
    out_ref[...] = acc[...].astype(BF16)


def expand(d, w, ids):
    rows, tile = d.shape[0], 512
    return pl.pallas_call(
        expand_kernel,
        grid=(rows // tile,),
        in_specs=[
            pl.BlockSpec((tile, 128), lambda i: (i, 0)),
            pl.BlockSpec(w.shape, lambda i: (0, 0)),
            pl.BlockSpec((tile, 2), lambda i: (i, 0)),
        ],
        out_specs=pl.BlockSpec((tile, HWIDE), lambda i: (i, 0)),
        out_shape=jax.ShapeDtypeStruct((rows, HWIDE), BF16),
        scratch_shapes=[pltpu.VMEM((tile, HWIDE), F32)],
        compiler_params=pltpu.CompilerParams(vmem_limit_bytes=VMEM),
        cost_estimate=pl.CostEstimate(
            flops=2 * rows * w.shape[0] * HWIDE,
            bytes_accessed=2 * (rows + w.shape[0]) * WIDTH,
            transcendentals=0,
        ),
        name="expand_entries",
    )(d, w, ids)


def router_term(specialist_pairs, weights, gates, dispatcher_map, experts):
    gate_val = gates.astype(jnp.float32)
    router_logit_gradient = weights * (
        gate_val - jnp.sum(weights * gate_val, axis=-1, keepdims=True)
    )
    ids = jnp.arange(experts, dtype=jnp.int32)
    expert_table = jnp.sum(
        jnp.where(
            specialist_pairs[:, :, None] == ids[None, None, :],
            router_logit_gradient[:, :, None],
            0.0,
        ),
        axis=1,
    )
    expert_table = expert_table.astype(jnp.bfloat16)
    term = jnp.einsum("te,de->td", expert_table, dispatcher_map, preferred_element_type=jnp.float32)
    return (router_logit_gradient, term)


def exchange(x, axes):
    return lax.all_to_all(x, axes, split_axis=0, concat_axis=0, tiled=True)


def local(
    hidden,
    output_gradient,
    specialist_pairs,
    chosen_router_logits,
    lowering_maps,
    raising_maps,
    dispatcher_map,
    queries,
    keys,
    values,
    context_gradient,
    query_projection,
    key_projection,
    value_projection,
    lengths,
):
    tok_rows = hidden.shape[0]
    width_d = output_gradient.shape[1]
    experts = 128
    tokens = tok_rows * SLICES
    columns = experts * RANK
    place = specialist_pairs % 8 * 16 + specialist_pairs // 8
    lane = jnp.arange(128, dtype=jnp.int32)[None, :]
    id_lanes = jnp.where(lane == 80, place[:, 0:1], jnp.where(lane == 81, place[:, 1:2], 0))
    w_mine = pack(lowering_maps[0].T, raising_maps[0], jnp.zeros((RANK, 128), F32))
    w_rows = exchange(w_mine, PLANE).reshape(SLICES * RANK, WIDTH)
    w_all = lax.all_gather(w_rows, LINE, axis=0, tiled=True)
    x_mine = pack(hidden, output_gradient, id_lanes.astype(F32))
    x = exchange(x_mine, PLANE).reshape(tokens, WIDTH)
    ids = x[:, 592:594].astype(jnp.int32)

    part = attend_backward(
        queries,
        keys,
        values,
        context_gradient,
        lengths[0],
        query_projection,
        key_projection,
        value_projection,
    ).astype(BF16)

    sums = contract(x, w_all, ids)
    sums = exchange(sums.reshape(SLICES, tok_rows, 128), PLANE).astype(F32)
    sums = jnp.sum(sums, axis=0)
    attention = exchange(part.reshape(8, tok_rows, width_d), TP)

    weights = jax.nn.softmax(chosen_router_logits, axis=-1)
    weights_b = weights.astype(BF16).astype(F32)
    sent, gates = [], []
    for k in range(2):
        z = sums[:, 64 * k : 64 * k + 32].astype(BF16).astype(F32)
        p = sums[:, 64 * k + 32 : 64 * k + 64]
        w = weights_b[:, k : k + 1]
        gates.append(jnp.sum(adapter_scale * z * p, axis=-1, keepdims=True).astype(BF16))
        sent.append((adapter_scale * w * p).astype(BF16))
        sent.append(adapter_scale * (w * z).astype(BF16))
    d = lax.all_gather(jnp.concatenate(sent, axis=1), PLANE, axis=0, tiled=True)
    gates = jnp.concatenate(gates, axis=1)

    factor_part = factors(x, d.T.astype(F32), jnp.pad(ids.T, ((0, 6), (0, 0))), columns)
    factor_rows = lax.psum_scatter(factor_part, LINE, scatter_dimension=0, tiled=True)
    hidden_part = expand(d, w_all, ids)
    hidden_back = exchange(hidden_part.reshape(SLICES, tok_rows, HWIDE), PLANE)
    factor_back = exchange(factor_rows.reshape(SLICES, RANK, WIDTH), PLANE)

    gated_hidden_gradient = unpack(hidden_back)
    down_factor_grad = unpack(factor_back).T
    up_main = factor_back[:, :, 640:768].transpose(1, 0, 2).reshape(RANK, 4096)
    up_rest = factor_back[:, :, 576:592].transpose(1, 0, 2).reshape(RANK, 512)
    up_factor_grad = jnp.concatenate([up_main, up_rest], axis=1)

    router_logit_gradient, term = router_term(
        specialist_pairs, weights, gates, dispatcher_map, experts
    )
    attention_rows = jnp.sum(attention.astype(F32), axis=0)
    residual_input_gradient = (output_gradient.astype(jnp.float32) + term + attention_rows).astype(
        jnp.bfloat16
    )
    return (
        residual_input_gradient,
        gated_hidden_gradient,
        router_logit_gradient,
        down_factor_grad[None],
        up_factor_grad[None],
    )


def solution(mesh):
    fine = Mesh(mesh.devices.reshape(4, 2, 2, 4, 2), ("y", "xl", "xh", "z", "c"))
    rows2, rows3, heads = P(ROWS, None), P(ROWS, None, None), P(EP, TP)
    in_specs = (
        rows2,
        rows2,
        rows2,
        rows2,
        rows3,
        rows3,
        P(),
        heads,
        heads,
        heads,
        heads,
        P(None, TP),
        P(None, TP),
        P(None, TP),
        P(EP, None),
    )
    out_specs = (rows2, rows2, rows2, rows3, rows3)
    return jax.shard_map(local, mesh=fine, in_specs=in_specs, out_specs=out_specs, check_vma=False)
```

```python
import jax
import jax.numpy as jnp
from jax import lax
from jax.experimental import pallas as pl
from jax.experimental.pallas import tpu as pltpu
from jax.sharding import Mesh, PartitionSpec as P

HD = 128
RANK = 32
PLANE = ("xl", "xh", "z", "c")
LINE = "y"
TP = ("y", "xl")
EP = ("xh", "z", "c")
ROWS = ("xh", "z", "c", "y", "xl")

SLICES = 32
WIDTH = 768
HWIDE = 640
PAIRS = 16
GROUPS = 16
PAIR_ROWS = 48
SLOTS = GROUPS * PAIR_ROWS
GROUP_ROWS = PAIRS * PAIR_ROWS
STEP = 2
UNROLL = 4

adapter_scale = 2.0
score_cap = 50.0
query_scale = 144.0 ** (-0.5)
F32 = jnp.float32
BF16 = jnp.bfloat16
VMEM = 60 * 1024 * 1024


def attend_backward(
    queries,
    keys,
    values,
    context_gradient,
    lengths,
    query_projection,
    key_projection,
    value_projection,
):
    rows = queries.shape[0]
    kv_count = keys.shape[1] // HD
    group = queries.shape[1] // keys.shape[1]
    query4 = queries.reshape(rows, kv_count, group, HD)
    ctx4 = context_gradient.reshape(rows, kv_count, group, HD)
    key3 = keys.reshape(rows, kv_count, HD)
    value3 = values.reshape(rows, kv_count, HD)
    places = jnp.arange(rows, dtype=jnp.int32)
    bounds = jnp.cumsum(lengths)
    docs = jnp.sum((places[:, None] >= bounds[None, :]).astype(jnp.int32), axis=1)
    allowed = (docs[:, None] == docs[None, :]) & (places[:, None] >= places[None, :])
    raw = (
        jnp.einsum("ikgd,jkd->kgij", query4, key3, preferred_element_type=jnp.float32) * query_scale
    )
    bent = jnp.tanh(raw / score_cap)
    expo = jnp.where(allowed, jnp.exp(score_cap * bent), 0.0)
    probs = expo / jnp.sum(expo, axis=-1, keepdims=True)
    dprobs = jnp.einsum("ikgd,jkd->kgij", ctx4, value3, preferred_element_type=jnp.float32)
    dsoft = probs * (dprobs - jnp.sum(probs * dprobs, axis=-1, keepdims=True))
    dscore = (dsoft * (1.0 - bent * bent)).astype(jnp.bfloat16)
    probs_b = probs.astype(jnp.bfloat16)
    dquery = (
        (
            jnp.einsum("kgij,jkd->ikgd", dscore, key3, preferred_element_type=jnp.float32)
            * query_scale
        )
        .astype(jnp.bfloat16)
        .reshape(rows, -1)
    )
    dkey = (
        (
            jnp.einsum("kgij,ikgd->jkd", dscore, query4, preferred_element_type=jnp.float32)
            * query_scale
        )
        .astype(jnp.bfloat16)
        .reshape(rows, -1)
    )
    dvalue = (
        jnp.einsum("kgij,ikgd->jkd", probs_b, ctx4, preferred_element_type=jnp.float32)
        .astype(jnp.bfloat16)
        .reshape(rows, -1)
    )
    grads = jnp.concatenate([dquery, dkey, dvalue], axis=1)
    maps = jnp.concatenate([query_projection, key_projection, value_projection], axis=1)
    return jnp.einsum("te,de->td", grads, maps, preferred_element_type=jnp.float32)


def lanes_of(shape):
    return lax.broadcasted_iota(jnp.int32, shape, len(shape) - 1)


def pack_kernel(hm_ref, hr_ref, gm_ref, gr_ref, id_ref, out_ref):
    rows = hm_ref.shape[0]
    lane = lanes_of((rows, 128))
    ids = id_ref[...]
    extra = gr_ref[...].astype(F32)
    extra = jnp.where(pl.program_id(0) % 2 == 0, extra, pltpu.roll(extra, 64, 1))
    for q in range(4):
        out_ref[q, :, 0:512] = hm_ref[:, 512 * q : 512 * q + 512]
        hid = hr_ref[:, 128 * (q // 2) : 128 * (q // 2) + 128].astype(F32)
        if q % 2:
            hid = pltpu.roll(hid, 64, 1)
        grad = pltpu.roll(extra, 64 - 16 * q, 1)
        tail = jnp.where(lane < 64, hid, jnp.where(lane < 80, grad, ids))
        out_ref[q, :, 512:640] = tail.astype(BF16)
        out_ref[q, :, 640:768] = gm_ref[:, 128 * q : 128 * q + 128]


def pack(hid, grad, ids):
    rows = hid.shape[0]
    return pl.pallas_call(
        pack_kernel,
        grid=(8,),
        in_specs=[
            pl.BlockSpec((rows, 2048), lambda i: (0, i)),
            pl.BlockSpec((rows, 256), lambda i: (0, 64 + i)),
            pl.BlockSpec((rows, 512), lambda i: (0, i)),
            pl.BlockSpec((rows, 128), lambda i: (0, 32 + i // 2)),
            pl.BlockSpec((rows, 128), lambda i: (0, 0)),
        ],
        out_specs=pl.BlockSpec((4, rows, WIDTH), lambda i: (i, 0, 0)),
        out_shape=jax.ShapeDtypeStruct((SLICES, rows, WIDTH), BF16),
        compiler_params=pltpu.CompilerParams(vmem_limit_bytes=VMEM),
        cost_estimate=pl.CostEstimate(
            flops=rows * 2 * 24576, bytes_accessed=rows * 2 * 49152, transcendentals=0
        ),
        name="pack_slices",
    )(hid, hid, grad, grad, ids)


def unpack_kernel(main_ref, rem_ref, out_ref):
    @pl.when(pl.program_id(0) < 8)
    def _():
        for q in range(4):
            out_ref[:, 512 * q : 512 * q + 512] = main_ref[q]

    @pl.when(pl.program_id(0) == 8)
    def _():
        lane = lanes_of(rem_ref.shape[1:])
        for d in range(16):
            low = rem_ref[2 * d].astype(F32)
            high = pltpu.roll(rem_ref[2 * d + 1].astype(F32), 64, 1)
            out_ref[:, 128 * d : 128 * d + 128] = jnp.where(lane < 64, low, high).astype(BF16)


def unpack(blocks):
    rows = blocks.shape[1]
    return pl.pallas_call(
        unpack_kernel,
        grid=(9,),
        in_specs=[
            pl.BlockSpec((4, rows, 512), lambda i: (jnp.minimum(i, 7), 0, 0)),
            pl.BlockSpec((SLICES, rows, 128), lambda i: (0, 0, 4)),
        ],
        out_specs=pl.BlockSpec((rows, 2048), lambda i: (0, i)),
        out_shape=jax.ShapeDtypeStruct((rows, 18432), BF16),
        compiler_params=pltpu.CompilerParams(vmem_limit_bytes=VMEM),
        cost_estimate=pl.CostEstimate(
            flops=rows * 18432, bytes_accessed=rows * 4 * 19000, transcendentals=0
        ),
        name="unpack_slices",
    )(blocks, blocks)


def hot(shape, axis, *slots):
    places = lax.broadcasted_iota(jnp.int32, shape, axis)
    found = places == slots[0]
    for s in slots[1:]:
        found = found | (places == s)
    return jnp.where(found, 1.0, 0.0).astype(BF16)


def slots_in_rows(tail):
    t = tail.astype(F32).T[80:88].astype(jnp.int32)
    second = jnp.where(lanes_of((1, 256)) >= 128, 3, 0)
    return [6 * t[k : k + 1] + t[2 + k : 3 + k] + second for k in range(2)]


def slots_in_columns(tail):
    t = tail.astype(F32)[:, 80:84].astype(jnp.int32)
    second = jnp.where(lax.broadcasted_iota(jnp.int32, (256, 1), 0) >= 128, 3, 0)
    return [6 * t[:, k : k + 1] + t[:, 2 + k : 3 + k] + second for k in range(2)]


def own_lanes(axis):
    shape = (GROUP_ROWS, 256) if axis == 0 else (256, GROUP_ROWS)
    slot = lax.broadcasted_iota(jnp.int32, shape, axis) % PAIR_ROWS // 6
    return slot == lax.broadcasted_iota(jnp.int32, shape, 1 - axis) // RANK


def repeat_lanes(k, axis):
    shape = (128, 256) if axis == 0 else (256, 128)
    a = lax.broadcasted_iota(jnp.int32, shape, axis)
    b = lax.broadcasted_iota(jnp.int32, shape, 1 - axis)
    return (a == b % RANK + RANK * k).astype(F32).astype(BF16)


def pair_at(q):
    return pl.ds(pl.multiple_of(q * 256, 256), 256)


def spread_pair(x):
    place = hot((SLOTS, 256), 0, *slots_in_rows(x[:, 512:640]))
    rows = jnp.dot(place, x, preferred_element_type=F32).astype(BF16)
    return rows.reshape(GROUPS, PAIR_ROWS, WIDTH)


def spread_kernel(x_ref, out_ref):
    for q in range(out_ref.shape[1]):
        out_ref[:, q] = spread_pair(x_ref[256 * q : 256 * q + 256])


def spread(x):
    return pl.pallas_call(
        spread_kernel,
        grid=(PAIRS // 2,),
        in_specs=[pl.BlockSpec((512, WIDTH), lambda i: (i, 0))],
        out_specs=pl.BlockSpec((GROUPS, 2, PAIR_ROWS, WIDTH), lambda i: (0, i, 0, 0)),
        out_shape=jax.ShapeDtypeStruct((GROUPS, PAIRS, PAIR_ROWS, WIDTH), BF16),
        compiler_params=pltpu.CompilerParams(vmem_limit_bytes=VMEM),
        cost_estimate=pl.CostEstimate(
            flops=2 * PAIRS * SLOTS * 256 * WIDTH,
            bytes_accessed=2 * PAIRS * (SLOTS + 256) * WIDTH,
            transcendentals=0,
        ),
        name="spread_rows",
    )(x)


def contract_kernel(x_ref, w_ref, out_ref, xs_ref, zs_ref):
    step = pl.program_id(0)

    @pl.when(step == 0)
    def _():
        def body(q, carry):
            xs_ref[:, q] = spread_pair(x_ref[pair_at(q)])
            return carry

        lax.fori_loop(0, PAIRS, body, 0, unroll=UNROLL)

    lane = lanes_of((256, 128))
    dims = (((1,), (1,)), ((), ()))
    mine = own_lanes(0)
    r = lax.broadcasted_iota(jnp.int32, (128, 128), 0) % RANK
    c = lax.broadcasted_iota(jnp.int32, (128, 128), 1)
    for n in range(STEP):
        group = step * STEP + n
        x = xs_ref[group].reshape(GROUP_ROWS, WIDTH)
        w = w_ref[256 * n : 256 * n + 256]
        tail = w[:, 512:640]
        zero = jnp.zeros_like(tail)
        w_h = jnp.concatenate([w[:, 0:512], jnp.where(lane < 64, tail, zero)], axis=1)
        w_g = jnp.concatenate([jnp.where(lane < 64, zero, tail), w[:, 640:768]], axis=1)
        out = jnp.zeros((GROUP_ROWS, 128), F32)
        for k, (w, cut) in enumerate(((w_h, slice(0, 640)), (w_g, slice(512, 768)))):
            full = lax.dot_general(x[:, cut], w, dims, preferred_element_type=F32)
            full = jnp.where(mine, full, 0.0)
            kept = (full[:, 0:128] + full[:, 128:256]).astype(BF16)
            fold = (c == r + RANK * k).astype(F32).astype(BF16)
            out += jnp.dot(kept, fold, preferred_element_type=F32)
        zs_ref[group] = out.astype(BF16).reshape(PAIRS, PAIR_ROWS, 128)

    @pl.when(step == GROUPS // STEP - 1)
    def _():
        half = lanes_of((256, 128))

        def body(q, carry):
            s0, s1 = slots_in_columns(x_ref[pair_at(q), 512:640])
            z = zs_ref[:, q].reshape(SLOTS, 128)
            first = jnp.dot(hot((256, SLOTS), 1, s0), z, preferred_element_type=F32)
            second = jnp.dot(hot((256, SLOTS), 1, s1), z, preferred_element_type=F32)
            out = jnp.where(half < 64, first, pltpu.roll(second, 64, 1))
            out_ref[pair_at(q)] = out.astype(BF16)
            return carry

        lax.fori_loop(0, PAIRS, body, 0, unroll=UNROLL)


def contract(x, w):
    return pl.pallas_call(
        contract_kernel,
        grid=(GROUPS // STEP,),
        in_specs=[
            pl.BlockSpec(x.shape, lambda i: (0, 0), pipeline_mode=pl.Buffered(1)),
            pl.BlockSpec((256 * STEP, WIDTH), lambda i: (i, 0)),
        ],
        out_specs=pl.BlockSpec((x.shape[0], 128), lambda i: (0, 0)),
        out_shape=jax.ShapeDtypeStruct((x.shape[0], 128), BF16),
        scratch_shapes=[
            pltpu.VMEM((GROUPS, PAIRS, PAIR_ROWS, WIDTH), BF16),
            pltpu.VMEM((GROUPS, PAIRS, PAIR_ROWS, 128), BF16),
        ],
        compiler_params=pltpu.CompilerParams(vmem_limit_bytes=VMEM),
        cost_estimate=pl.CostEstimate(
            flops=2 * GROUPS * GROUP_ROWS * 256 * 1024,
            bytes_accessed=4 * x.shape[0] * WIDTH,
            transcendentals=0,
        ),
        name="contract_experts",
    )(x, w)


def place_latents(t_ref, d_ref, ds_ref):
    half = lanes_of((256, 128))

    def body(q, carry):
        s0, s1 = slots_in_rows(t_ref[pair_at(q)])
        d = d_ref[pair_at(q)].astype(F32)
        d0 = jnp.where(half < 64, d, 0.0).astype(BF16)
        d1 = jnp.where(half < 64, pltpu.roll(d, 64, 1), 0.0).astype(BF16)
        rows = jnp.dot(hot((SLOTS, 256), 0, s0), d0, preferred_element_type=F32)
        rows += jnp.dot(hot((SLOTS, 256), 0, s1), d1, preferred_element_type=F32)
        ds_ref[:, q] = rows.astype(BF16).reshape(GROUPS, PAIR_ROWS, 128)
        return carry

    lax.fori_loop(0, PAIRS, body, 0, unroll=UNROLL)


def gradients_kernel(t_ref, d_ref, x_ref, w_ref, factor_ref, hidden_ref, ds_ref, gs_ref):
    step = pl.program_id(0)

    @pl.when(step == 0)
    def _():
        place_latents(t_ref, d_ref, ds_ref)

    dims = (((1,), (1,)), ((), ()))
    across, along = own_lanes(0), own_lanes(1)
    for n in range(STEP):
        group = step * STEP + n
        x = x_ref[n].reshape(GROUP_ROWS, WIDTH)
        d = ds_ref[group].reshape(GROUP_ROWS, 128)
        outs = []
        for k, cut in ((0, slice(0, 640)), (1, slice(512, 768))):
            wide = lax.dot_general(repeat_lanes(k, 1), d, dims, preferred_element_type=F32)
            wide = jnp.where(along, wide, 0.0).astype(BF16)
            outs.append(jnp.dot(wide, x[:, cut], preferred_element_type=F32))
        hid, grad = outs
        at = slice(256 * n, 256 * n + 256)
        factor_ref[at, 0:512] = hid[:, 0:512].astype(BF16)
        tail = jnp.where(lanes_of((256, 128)) < 64, hid[:, 512:640], grad[:, 0:128])
        factor_ref[at, 512:640] = tail.astype(BF16)
        factor_ref[at, 640:768] = grad[:, 128:256].astype(BF16)
        wide = jnp.dot(d, repeat_lanes(0, 0), preferred_element_type=F32)
        wide = jnp.where(across, wide, 0.0).astype(BF16)
        out = jnp.dot(wide, w_ref[at, 0:640], preferred_element_type=F32).astype(BF16)
        gs_ref[group] = out.reshape(PAIRS, PAIR_ROWS, HWIDE)

    @pl.when(step == GROUPS // STEP - 1)
    def _():
        def body(q, carry):
            both = hot((256, SLOTS), 1, *slots_in_columns(t_ref[pair_at(q)]))
            g = gs_ref[:, q].reshape(SLOTS, HWIDE)
            hidden_ref[pair_at(q)] = jnp.dot(both, g, preferred_element_type=F32).astype(BF16)
            return carry

        lax.fori_loop(0, PAIRS, body, 0, unroll=UNROLL)


def gradients(x, d, xs, w):
    rows = x.shape[0]
    once = pl.Buffered(1)
    return pl.pallas_call(
        gradients_kernel,
        grid=(GROUPS // STEP,),
        in_specs=[
            pl.BlockSpec((rows, 128), lambda i: (0, 4), pipeline_mode=once),
            pl.BlockSpec((rows, 128), lambda i: (0, 0), pipeline_mode=once),
            pl.BlockSpec((STEP, PAIRS, PAIR_ROWS, WIDTH), lambda i: (i, 0, 0, 0)),
            pl.BlockSpec((256 * STEP, WIDTH), lambda i: (i, 0)),
        ],
        out_specs=[
            pl.BlockSpec((256 * STEP, WIDTH), lambda i: (i, 0)),
            pl.BlockSpec((rows, HWIDE), lambda i: (0, 0), pipeline_mode=once),
        ],
        out_shape=[
            jax.ShapeDtypeStruct((GROUPS * 256, WIDTH), BF16),
            jax.ShapeDtypeStruct((rows, HWIDE), BF16),
        ],
        scratch_shapes=[
            pltpu.VMEM((GROUPS, PAIRS, PAIR_ROWS, 128), BF16),
            pltpu.VMEM((GROUPS, PAIRS, PAIR_ROWS, HWIDE), BF16),
        ],
        compiler_params=pltpu.CompilerParams(vmem_limit_bytes=VMEM),
        cost_estimate=pl.CostEstimate(
            flops=4 * GROUPS * GROUP_ROWS * 256 * 1024,
            bytes_accessed=2 * GROUPS * GROUP_ROWS * WIDTH + 8 * rows * WIDTH,
            transcendentals=0,
        ),
        name="factor_and_hidden_gradients",
    )(x, d, xs, w)


def router_term(specialist_pairs, weights, gates, dispatcher_map, experts):
    gate_val = gates.astype(jnp.float32)
    router_logit_gradient = weights * (
        gate_val - jnp.sum(weights * gate_val, axis=-1, keepdims=True)
    )
    ids = jnp.arange(experts, dtype=jnp.int32)
    expert_table = jnp.sum(
        jnp.where(
            specialist_pairs[:, :, None] == ids[None, None, :],
            router_logit_gradient[:, :, None],
            0.0,
        ),
        axis=1,
    )
    expert_table = expert_table.astype(jnp.bfloat16)
    term = jnp.einsum("te,de->td", expert_table, dispatcher_map, preferred_element_type=jnp.float32)
    return (router_logit_gradient, term)


def exchange(x, axes):
    return lax.all_to_all(x, axes, split_axis=0, concat_axis=0, tiled=True)


def local(
    hidden,
    output_gradient,
    specialist_pairs,
    chosen_router_logits,
    lowering_maps,
    raising_maps,
    dispatcher_map,
    queries,
    keys,
    values,
    context_gradient,
    query_projection,
    key_projection,
    value_projection,
    lengths,
):
    tok_rows = hidden.shape[0]
    width_d = output_gradient.shape[1]
    experts = 128
    tokens = tok_rows * SLICES
    place = specialist_pairs % 8 * 16 + specialist_pairs // 8
    lane = jnp.arange(128, dtype=jnp.int32)[None, :]
    named = (place[:, :, None] == lane[None]).astype(F32)
    earlier = jnp.tril(jnp.ones((tok_rows, tok_rows), BF16), -1)
    before = jnp.dot(earlier, jnp.sum(named, axis=1).astype(BF16), preferred_element_type=F32)
    rank = jnp.sum(named * before[:, None, :], axis=2)
    id_lanes = jnp.zeros((tok_rows, 128), F32)
    for at, column in enumerate((place[:, 0], place[:, 1], rank[:, 0], rank[:, 1])):
        id_lanes = jnp.where(lane == 80 + at, column.astype(F32)[:, None], id_lanes)
    w_mine = pack(lowering_maps[0].T, raising_maps[0], jnp.zeros((RANK, 128), F32))
    x_mine = pack(hidden, output_gradient, id_lanes)
    w_rows = exchange(w_mine, PLANE)
    w_rows, x_mine = lax.optimization_barrier((w_rows, x_mine))
    w_all = lax.all_gather(w_rows.reshape(SLICES * RANK, WIDTH), LINE, axis=0, tiled=True)
    x = exchange(x_mine, PLANE).reshape(tokens, WIDTH)

    part = attend_backward(
        queries,
        keys,
        values,
        context_gradient,
        lengths[0],
        query_projection,
        key_projection,
        value_projection,
    ).astype(BF16)

    x, part = lax.optimization_barrier((x, part))
    part_rows = lax.psum_scatter(part, LINE, scatter_dimension=0, tiled=True)
    sums = contract(x, w_all)
    x, sums = lax.optimization_barrier((x, sums))
    xs = spread(x)
    sums = exchange(sums.reshape(SLICES, tok_rows, 128), PLANE)
    xs, sums, part_rows = lax.optimization_barrier((xs, sums, part_rows))
    sums = jnp.sum(sums.astype(F32), axis=0)
    side = lax.axis_index("xl")
    halves = part_rows.reshape(2, tok_rows, width_d)
    kept = lax.dynamic_index_in_dim(halves, side, 0, keepdims=False)
    passed = lax.dynamic_index_in_dim(halves, 1 - side, 0, keepdims=False)
    passed = lax.ppermute(passed, "xl", [(0, 1), (1, 0)])

    weights = jax.nn.softmax(chosen_router_logits, axis=-1)
    weights_b = weights.astype(BF16).astype(F32)
    sent, gates = [], []
    for k in range(2):
        z = sums[:, 64 * k : 64 * k + 32].astype(BF16).astype(F32)
        p = sums[:, 64 * k + 32 : 64 * k + 64]
        w = weights_b[:, k : k + 1]
        gates.append(jnp.sum(adapter_scale * z * p, axis=-1, keepdims=True).astype(BF16))
        sent.append((adapter_scale * w * p).astype(BF16))
        sent.append(adapter_scale * (w * z).astype(BF16))
    mine = jnp.concatenate(sent, axis=1)
    d = exchange(jnp.broadcast_to(mine[None], (SLICES,) + mine.shape), PLANE)
    gates = jnp.concatenate(gates, axis=1)

    d = d.reshape(tokens, 128)
    factor_part, hidden_part = gradients(x, d, xs, w_all)
    factor_rows = lax.psum_scatter(factor_part, LINE, scatter_dimension=0, tiled=True)
    hidden_back = exchange(hidden_part.reshape(SLICES, tok_rows, HWIDE), PLANE)
    factor_back = exchange(factor_rows.reshape(SLICES, RANK, WIDTH), PLANE)

    gated_hidden_gradient = unpack(hidden_back)
    down_factor_grad = unpack(factor_back).T
    up_main = factor_back[:, :, 640:768].transpose(1, 0, 2).reshape(RANK, 4096)
    up_rest = factor_back[:, :, 576:592].transpose(1, 0, 2).reshape(RANK, 512)
    up_factor_grad = jnp.concatenate([up_main, up_rest], axis=1)

    router_logit_gradient, term = router_term(
        specialist_pairs, weights, gates, dispatcher_map, experts
    )
    attention_rows = kept.astype(F32) + passed.astype(F32)
    residual_input_gradient = (output_gradient.astype(jnp.float32) + term + attention_rows).astype(
        jnp.bfloat16
    )
    return (
        residual_input_gradient,
        gated_hidden_gradient,
        router_logit_gradient,
        down_factor_grad[None],
        up_factor_grad[None],
    )


def solution(mesh):
    fine = Mesh(mesh.devices.reshape(4, 2, 2, 4, 2), ("y", "xl", "xh", "z", "c"))
    rows2, rows3, heads = P(ROWS, None), P(ROWS, None, None), P(EP, TP)
    in_specs = (
        rows2,
        rows2,
        rows2,
        rows2,
        rows3,
        rows3,
        P(),
        heads,
        heads,
        heads,
        heads,
        P(None, TP),
        P(None, TP),
        P(None, TP),
        P(EP, None),
    )
    out_specs = (rows2, rows2, rows2, rows3, rows3)
    return jax.shard_map(local, mesh=fine, in_specs=in_specs, out_specs=out_specs, check_vma=False)
```

```python
import jax
import jax.numpy as jnp
from jax import lax
from jax.experimental import pallas as pl
from jax.experimental.pallas import tpu as pltpu
from jax.sharding import Mesh, PartitionSpec as P

HD = 128
RANK = 32
PLANE = ("xl", "xh", "z", "c")
LINE = "y"
TP = ("y", "xl")
EP = ("xh", "z", "c")
ROWS = ("xh", "z", "c", "y", "xl")

SLICES = 32
WIDTH = 768
HWIDE = 640
PAIRS = 16
GROUPS = 16
PAIR_ROWS = 48
SLOTS = GROUPS * PAIR_ROWS
GROUP_ROWS = PAIRS * PAIR_ROWS
STEP = 4
UNROLL = 4

adapter_scale = 2.0
score_cap = 50.0
query_scale = 144.0 ** (-0.5)
F32 = jnp.float32
BF16 = jnp.bfloat16
VMEM = 60 * 1024 * 1024


def attend_scores(queries, keys, lengths):
    rows = queries.shape[0]
    kv_count = keys.shape[1] // HD
    group = queries.shape[1] // keys.shape[1]
    query4 = queries.reshape(rows, kv_count, group, HD)
    key3 = keys.reshape(rows, kv_count, HD)
    places = jnp.arange(rows, dtype=jnp.int32)
    bounds = jnp.cumsum(lengths)
    docs = jnp.sum((places[:, None] >= bounds[None, :]).astype(jnp.int32), axis=1)
    allowed = (docs[:, None] == docs[None, :]) & (places[:, None] >= places[None, :])
    raw = (
        jnp.einsum("ikgd,jkd->kgij", query4, key3, preferred_element_type=jnp.float32) * query_scale
    )
    expo = jnp.where(allowed, jnp.exp(score_cap * jnp.tanh(raw / score_cap)), 0.0)
    return raw, jnp.sum(expo, axis=-1, keepdims=True), allowed


def attend_backward(
    raw,
    total,
    allowed,
    queries,
    keys,
    values,
    context_gradient,
    query_projection,
    key_projection,
    value_projection,
):
    rows = queries.shape[0]
    kv_count = keys.shape[1] // HD
    group = queries.shape[1] // keys.shape[1]
    query4 = queries.reshape(rows, kv_count, group, HD)
    ctx4 = context_gradient.reshape(rows, kv_count, group, HD)
    key3 = keys.reshape(rows, kv_count, HD)
    value3 = values.reshape(rows, kv_count, HD)
    bent = jnp.tanh(raw / score_cap)
    expo = jnp.where(allowed, jnp.exp(score_cap * bent), 0.0)
    probs = expo / total
    dprobs = jnp.einsum("ikgd,jkd->kgij", ctx4, value3, preferred_element_type=jnp.float32)
    dsoft = probs * (dprobs - jnp.sum(probs * dprobs, axis=-1, keepdims=True))
    dscore = (dsoft * (1.0 - bent * bent)).astype(jnp.bfloat16)
    probs_b = probs.astype(jnp.bfloat16)
    dquery = (
        (
            jnp.einsum("kgij,jkd->ikgd", dscore, key3, preferred_element_type=jnp.float32)
            * query_scale
        )
        .astype(jnp.bfloat16)
        .reshape(rows, -1)
    )
    dkey = (
        (
            jnp.einsum("kgij,ikgd->jkd", dscore, query4, preferred_element_type=jnp.float32)
            * query_scale
        )
        .astype(jnp.bfloat16)
        .reshape(rows, -1)
    )
    dvalue = (
        jnp.einsum("kgij,ikgd->jkd", probs_b, ctx4, preferred_element_type=jnp.float32)
        .astype(jnp.bfloat16)
        .reshape(rows, -1)
    )
    grads = jnp.concatenate([dquery, dkey, dvalue], axis=1)
    maps = jnp.concatenate([query_projection, key_projection, value_projection], axis=1)
    return jnp.einsum("te,de->td", grads, maps, preferred_element_type=jnp.float32)


def lanes_of(shape):
    return lax.broadcasted_iota(jnp.int32, shape, len(shape) - 1)


def pack_kernel(hm_ref, hr_ref, gm_ref, gr_ref, id_ref, out_ref):
    rows = hm_ref.shape[0]
    lane = lanes_of((rows, 128))
    ids = id_ref[...]
    for q in range(8):
        out_ref[q, :, 0:512] = hm_ref[:, 512 * q : 512 * q + 512]
        hid = hr_ref[:, 128 * (q // 2) : 128 * (q // 2) + 128].astype(F32)
        if q % 2:
            hid = pltpu.roll(hid, 64, 1)
        grad = pltpu.roll(gr_ref[...].astype(F32), (64 - 16 * q) % 128, 1)
        tail = jnp.where(lane < 64, hid, jnp.where(lane < 80, grad, ids))
        out_ref[q, :, 512:640] = tail.astype(BF16)
        out_ref[q, :, 640:768] = gm_ref[:, 128 * q : 128 * q + 128]


def pack(hid, grad, ids):
    rows = hid.shape[0]
    return pl.pallas_call(
        pack_kernel,
        grid=(4,),
        in_specs=[
            pl.BlockSpec((rows, 4096), lambda i: (0, i)),
            pl.BlockSpec((rows, 512), lambda i: (0, 32 + i)),
            pl.BlockSpec((rows, 1024), lambda i: (0, i)),
            pl.BlockSpec((rows, 128), lambda i: (0, 32 + i)),
            pl.BlockSpec((rows, 128), lambda i: (0, 0)),
        ],
        out_specs=pl.BlockSpec((8, rows, WIDTH), lambda i: (i, 0, 0)),
        out_shape=jax.ShapeDtypeStruct((SLICES, rows, WIDTH), BF16),
        compiler_params=pltpu.CompilerParams(vmem_limit_bytes=VMEM),
        cost_estimate=pl.CostEstimate(
            flops=rows * 2 * 24576, bytes_accessed=rows * 2 * 49152, transcendentals=0
        ),
        name="pack_slices",
    )(hid, hid, grad, grad, ids)


def unpack_kernel(main_ref, rem_ref, out_ref):
    step = pl.program_id(0)

    @pl.when(step < 4)
    def _():
        for q in range(8):
            out_ref[:, 512 * q : 512 * q + 512] = main_ref[q]

    @pl.when(step == 4)
    def _():
        lane = lanes_of(rem_ref.shape[1:])
        for d in range(16):
            low = rem_ref[2 * d].astype(F32)
            high = pltpu.roll(rem_ref[2 * d + 1].astype(F32), 64, 1)
            out_ref[:, 128 * d : 128 * d + 128] = jnp.where(lane < 64, low, high).astype(BF16)


def unpack(blocks):
    rows = blocks.shape[1]
    return pl.pallas_call(
        unpack_kernel,
        grid=(5,),
        in_specs=[
            pl.BlockSpec((8, rows, 512), lambda i: (jnp.minimum(i, 3), 0, 0)),
            pl.BlockSpec((SLICES, rows, 128), lambda i: (0, 0, 4), pipeline_mode=pl.Buffered(1)),
        ],
        out_specs=pl.BlockSpec((rows, 4096), lambda i: (0, i)),
        out_shape=jax.ShapeDtypeStruct((rows, 18432), BF16),
        compiler_params=pltpu.CompilerParams(vmem_limit_bytes=VMEM),
        cost_estimate=pl.CostEstimate(
            flops=rows * 18432, bytes_accessed=rows * 4 * 19000, transcendentals=0
        ),
        name="unpack_slices",
    )(blocks, blocks)


def hot(shape, axis, *slots):
    places = lax.broadcasted_iota(jnp.int32, shape, axis)
    found = places == slots[0]
    for s in slots[1:]:
        found = found | (places == s)
    return jnp.where(found, 1.0, 0.0).astype(BF16)


def slots_in_rows(tail):
    t = tail.astype(F32).T[80:88].astype(jnp.int32)
    second = jnp.where(lanes_of((1, 256)) >= 128, 3, 0)
    return [6 * t[k : k + 1] + t[2 + k : 3 + k] + second for k in range(2)]


def slots_in_columns(tail):
    t = tail.astype(F32)[:, 80:84].astype(jnp.int32)
    second = jnp.where(lax.broadcasted_iota(jnp.int32, (256, 1), 0) >= 128, 3, 0)
    return [6 * t[:, k : k + 1] + t[:, 2 + k : 3 + k] + second for k in range(2)]


def own_lanes(axis):
    shape = (GROUP_ROWS, 256) if axis == 0 else (256, GROUP_ROWS)
    slot = lax.broadcasted_iota(jnp.int32, shape, axis) % PAIR_ROWS // 6
    return slot == lax.broadcasted_iota(jnp.int32, shape, 1 - axis) // RANK


def repeat_lanes(k, axis):
    shape = (128, 256) if axis == 0 else (256, 128)
    a = lax.broadcasted_iota(jnp.int32, shape, axis)
    b = lax.broadcasted_iota(jnp.int32, shape, 1 - axis)
    return (a == b % RANK + RANK * k).astype(F32).astype(BF16)


def pair_at(q):
    return pl.ds(pl.multiple_of(q * 256, 256), 256)


def spread_pair(x):
    place = hot((SLOTS, 256), 0, *slots_in_rows(x[:, 512:640]))
    rows = jnp.dot(place, x, preferred_element_type=F32).astype(BF16)
    return rows.reshape(GROUPS, PAIR_ROWS, WIDTH)


def spread_kernel(x_ref, out_ref):
    for q in range(out_ref.shape[1]):
        out_ref[:, q] = spread_pair(x_ref[256 * q : 256 * q + 256])


def spread(x):
    return pl.pallas_call(
        spread_kernel,
        grid=(PAIRS // 2,),
        in_specs=[pl.BlockSpec((512, WIDTH), lambda i: (i, 0))],
        out_specs=pl.BlockSpec((GROUPS, 2, PAIR_ROWS, WIDTH), lambda i: (0, i, 0, 0)),
        out_shape=jax.ShapeDtypeStruct((GROUPS, PAIRS, PAIR_ROWS, WIDTH), BF16),
        compiler_params=pltpu.CompilerParams(vmem_limit_bytes=VMEM),
        cost_estimate=pl.CostEstimate(
            flops=2 * PAIRS * SLOTS * 256 * WIDTH,
            bytes_accessed=2 * PAIRS * (SLOTS + 256) * WIDTH,
            transcendentals=0,
        ),
        name="spread_rows",
    )(x)


def contract_kernel(x_ref, w_ref, out_ref, xs_ref, zs_ref):
    step = pl.program_id(0)

    @pl.when(step == 0)
    def _():
        def body(q, carry):
            xs_ref[:, q] = spread_pair(x_ref[pair_at(q)])
            return carry

        lax.fori_loop(0, PAIRS, body, 0, unroll=UNROLL)

    lane = lanes_of((256, 128))
    dims = (((1,), (1,)), ((), ()))
    mine = own_lanes(0)
    r = lax.broadcasted_iota(jnp.int32, (128, 128), 0) % RANK
    c = lax.broadcasted_iota(jnp.int32, (128, 128), 1)
    for n in range(STEP):
        group = step * STEP + n
        x = xs_ref[group].reshape(GROUP_ROWS, WIDTH)
        w = w_ref[256 * n : 256 * n + 256]
        tail = w[:, 512:640]
        zero = jnp.zeros_like(tail)
        w_h = jnp.concatenate([w[:, 0:512], jnp.where(lane < 64, tail, zero)], axis=1)
        w_g = jnp.concatenate([jnp.where(lane < 64, zero, tail), w[:, 640:768]], axis=1)
        out = jnp.zeros((GROUP_ROWS, 128), F32)
        for k, (w, cut) in enumerate(((w_h, slice(0, 640)), (w_g, slice(512, 768)))):
            full = lax.dot_general(x[:, cut], w, dims, preferred_element_type=F32)
            full = jnp.where(mine, full, 0.0)
            kept = (full[:, 0:128] + full[:, 128:256]).astype(BF16)
            fold = (c == r + RANK * k).astype(F32).astype(BF16)
            out += jnp.dot(kept, fold, preferred_element_type=F32)
        zs_ref[group] = out.astype(BF16).reshape(PAIRS, PAIR_ROWS, 128)

    @pl.when(step == GROUPS // STEP - 1)
    def _():
        half = lanes_of((256, 128))

        def body(q, carry):
            s0, s1 = slots_in_columns(x_ref[pair_at(q), 512:640])
            z = zs_ref[:, q].reshape(SLOTS, 128)
            place = hot((512, SLOTS), 1, jnp.concatenate([s0, s1], axis=0))
            found = jnp.dot(place, z, preferred_element_type=F32)
            out = jnp.where(half < 64, found[0:256], pltpu.roll(found[256:512], 64, 1))
            out_ref[pair_at(q)] = out.astype(BF16)
            return carry

        lax.fori_loop(0, PAIRS, body, 0, unroll=UNROLL)


def contract(x, w):
    return pl.pallas_call(
        contract_kernel,
        grid=(GROUPS // STEP,),
        in_specs=[
            pl.BlockSpec(x.shape, lambda i: (0, 0), pipeline_mode=pl.Buffered(1)),
            pl.BlockSpec((256 * STEP, WIDTH), lambda i: (i, 0)),
        ],
        out_specs=pl.BlockSpec((x.shape[0], 128), lambda i: (0, 0)),
        out_shape=jax.ShapeDtypeStruct((x.shape[0], 128), BF16),
        scratch_shapes=[
            pltpu.VMEM((GROUPS, PAIRS, PAIR_ROWS, WIDTH), BF16),
            pltpu.VMEM((GROUPS, PAIRS, PAIR_ROWS, 128), BF16),
        ],
        compiler_params=pltpu.CompilerParams(vmem_limit_bytes=VMEM),
        cost_estimate=pl.CostEstimate(
            flops=2 * GROUPS * GROUP_ROWS * 256 * 1024,
            bytes_accessed=4 * x.shape[0] * WIDTH,
            transcendentals=0,
        ),
        name="contract_experts",
    )(x, w)


def place_latents(t_ref, d_ref, ds_ref):
    half = lanes_of((256, 128))

    def body(q, carry):
        s0, s1 = slots_in_rows(t_ref[pair_at(q)])
        d = d_ref[pair_at(q)].astype(F32)
        d0 = jnp.where(half < 64, d, 0.0).astype(BF16)
        d1 = jnp.where(half < 64, pltpu.roll(d, 64, 1), 0.0).astype(BF16)
        place = hot((SLOTS, 512), 0, jnp.concatenate([s0, s1], axis=1))
        rows = jnp.dot(place, jnp.concatenate([d0, d1], axis=0), preferred_element_type=F32)
        ds_ref[:, q] = rows.astype(BF16).reshape(GROUPS, PAIR_ROWS, 128)
        return carry

    lax.fori_loop(0, PAIRS, body, 0, unroll=UNROLL)


def gradients_kernel(t_ref, d_ref, x_ref, w_ref, factor_ref, hidden_ref, ds_ref, gs_ref):
    step = pl.program_id(0)

    @pl.when(step == 0)
    def _():
        place_latents(t_ref, d_ref, ds_ref)

    dims = (((1,), (1,)), ((), ()))
    across, along = own_lanes(0), own_lanes(1)
    for n in range(STEP):
        group = step * STEP + n
        x = x_ref[n].reshape(GROUP_ROWS, WIDTH)
        d = ds_ref[group].reshape(GROUP_ROWS, 128)
        outs = []
        for k, cut in ((0, slice(0, 640)), (1, slice(512, 768))):
            wide = lax.dot_general(repeat_lanes(k, 1), d, dims, preferred_element_type=F32)
            wide = jnp.where(along, wide, 0.0).astype(BF16)
            outs.append(jnp.dot(wide, x[:, cut], preferred_element_type=F32))
        hid, grad = outs
        at = slice(256 * n, 256 * n + 256)
        factor_ref[at, 0:512] = hid[:, 0:512].astype(BF16)
        tail = jnp.where(lanes_of((256, 128)) < 64, hid[:, 512:640], grad[:, 0:128])
        factor_ref[at, 512:640] = tail.astype(BF16)
        factor_ref[at, 640:768] = grad[:, 128:256].astype(BF16)
        wide = jnp.dot(d, repeat_lanes(0, 0), preferred_element_type=F32)
        wide = jnp.where(across, wide, 0.0).astype(BF16)
        out = jnp.dot(wide, w_ref[at, 0:640], preferred_element_type=F32).astype(BF16)
        gs_ref[group] = out.reshape(PAIRS, PAIR_ROWS, HWIDE)

    @pl.when(step == GROUPS // STEP - 1)
    def _():
        def body(q, carry):
            both = hot((256, SLOTS), 1, *slots_in_columns(t_ref[pair_at(q)]))
            g = gs_ref[:, q].reshape(SLOTS, HWIDE)
            hidden_ref[pair_at(q)] = jnp.dot(both, g, preferred_element_type=F32).astype(BF16)
            return carry

        lax.fori_loop(0, PAIRS, body, 0, unroll=UNROLL)


def gradients(x, d, xs, w):
    rows = x.shape[0]
    once = pl.Buffered(1)
    return pl.pallas_call(
        gradients_kernel,
        grid=(GROUPS // STEP,),
        in_specs=[
            pl.BlockSpec((rows, 128), lambda i: (0, 4), pipeline_mode=once),
            pl.BlockSpec((rows, 128), lambda i: (0, 0), pipeline_mode=once),
            pl.BlockSpec((STEP, PAIRS, PAIR_ROWS, WIDTH), lambda i: (i, 0, 0, 0)),
            pl.BlockSpec((256 * STEP, WIDTH), lambda i: (i, 0)),
        ],
        out_specs=[
            pl.BlockSpec((256 * STEP, WIDTH), lambda i: (i, 0)),
            pl.BlockSpec((rows, HWIDE), lambda i: (0, 0), pipeline_mode=once),
        ],
        out_shape=[
            jax.ShapeDtypeStruct((GROUPS * 256, WIDTH), BF16),
            jax.ShapeDtypeStruct((rows, HWIDE), BF16),
        ],
        scratch_shapes=[
            pltpu.VMEM((GROUPS, PAIRS, PAIR_ROWS, 128), BF16),
            pltpu.VMEM((GROUPS, PAIRS, PAIR_ROWS, HWIDE), BF16),
        ],
        compiler_params=pltpu.CompilerParams(vmem_limit_bytes=VMEM),
        cost_estimate=pl.CostEstimate(
            flops=4 * GROUPS * GROUP_ROWS * 256 * 1024,
            bytes_accessed=2 * GROUPS * GROUP_ROWS * WIDTH + 8 * rows * WIDTH,
            transcendentals=0,
        ),
        name="factor_and_hidden_gradients",
    )(x, d, xs, w)


def router_term(specialist_pairs, weights, gates, dispatcher_map, experts):
    gate_val = gates.astype(jnp.float32)
    router_logit_gradient = weights * (
        gate_val - jnp.sum(weights * gate_val, axis=-1, keepdims=True)
    )
    ids = jnp.arange(experts, dtype=jnp.int32)
    expert_table = jnp.sum(
        jnp.where(
            specialist_pairs[:, :, None] == ids[None, None, :],
            router_logit_gradient[:, :, None],
            0.0,
        ),
        axis=1,
    )
    expert_table = expert_table.astype(jnp.bfloat16)
    term = jnp.einsum("te,de->td", expert_table, dispatcher_map, preferred_element_type=jnp.float32)
    return (router_logit_gradient, term)


def exchange(x, axes):
    return lax.all_to_all(x, axes, split_axis=0, concat_axis=0, tiled=True)


def local(
    hidden,
    output_gradient,
    specialist_pairs,
    chosen_router_logits,
    lowering_maps,
    raising_maps,
    dispatcher_map,
    queries,
    keys,
    values,
    context_gradient,
    query_projection,
    key_projection,
    value_projection,
    lengths,
):
    tok_rows = hidden.shape[0]
    width_d = output_gradient.shape[1]
    experts = 128
    tokens = tok_rows * SLICES
    place = specialist_pairs % 8 * 16 + specialist_pairs // 8
    lane = jnp.arange(128, dtype=jnp.int32)[None, :]
    named = (place[:, :, None] == lane[None]).astype(F32)
    earlier = jnp.tril(jnp.ones((tok_rows, tok_rows), BF16), -1)
    before = jnp.dot(earlier, jnp.sum(named, axis=1).astype(BF16), preferred_element_type=F32)
    rank = jnp.sum(named * before[:, None, :], axis=2)
    id_lanes = jnp.zeros((tok_rows, 128), F32)
    for at, column in enumerate((place[:, 0], place[:, 1], rank[:, 0], rank[:, 1])):
        id_lanes = jnp.where(lane == 80 + at, column.astype(F32)[:, None], id_lanes)
    w_mine = pack(lowering_maps[0].T, raising_maps[0], jnp.zeros((RANK, 128), F32))
    x_mine = pack(hidden, output_gradient, id_lanes)
    w_rows = exchange(w_mine, PLANE)
    scores = attend_scores(queries, keys, lengths[0])
    w_rows, x_mine, scores = lax.optimization_barrier((w_rows, x_mine, scores))
    w_all = lax.all_gather(w_rows.reshape(SLICES * RANK, WIDTH), LINE, axis=0, tiled=True)
    x = exchange(x_mine, PLANE).reshape(tokens, WIDTH)

    part = attend_backward(
        *scores,
        queries,
        keys,
        values,
        context_gradient,
        query_projection,
        key_projection,
        value_projection,
    ).astype(BF16)

    part_rows = lax.psum_scatter(part, LINE, scatter_dimension=0, tiled=True)
    x, _ = lax.optimization_barrier((x, part))
    sums = contract(x, w_all)
    x, sums = lax.optimization_barrier((x, sums))
    xs = spread(x)
    sums = exchange(sums.reshape(SLICES, tok_rows, 128), PLANE)
    xs, sums, part_rows = lax.optimization_barrier((xs, sums, part_rows))
    sums = jnp.sum(sums.astype(F32), axis=0)
    side = lax.axis_index("xl")
    halves = part_rows.reshape(2, tok_rows, width_d)
    kept = lax.dynamic_index_in_dim(halves, side, 0, keepdims=False)
    passed = lax.dynamic_index_in_dim(halves, 1 - side, 0, keepdims=False)
    passed = lax.ppermute(passed, "xl", [(0, 1), (1, 0)])

    weights = jax.nn.softmax(chosen_router_logits, axis=-1)
    weights_b = weights.astype(BF16).astype(F32)
    sent, gates = [], []
    for k in range(2):
        z = sums[:, 64 * k : 64 * k + 32].astype(BF16).astype(F32)
        p = sums[:, 64 * k + 32 : 64 * k + 64]
        w = weights_b[:, k : k + 1]
        gates.append(jnp.sum(adapter_scale * z * p, axis=-1, keepdims=True).astype(BF16))
        sent.append((adapter_scale * w * p).astype(BF16))
        sent.append(adapter_scale * (w * z).astype(BF16))
    mine = jnp.concatenate(sent, axis=1)
    d = exchange(jnp.broadcast_to(mine[None], (SLICES,) + mine.shape), PLANE)
    gates = jnp.concatenate(gates, axis=1)

    d = d.reshape(tokens, 128)
    factor_part, hidden_part = gradients(x, d, xs, w_all)
    hidden_part, passed = lax.optimization_barrier((hidden_part, passed))
    factor_rows = lax.psum_scatter(factor_part, LINE, scatter_dimension=0, tiled=True)
    hidden_back = exchange(hidden_part.reshape(SLICES, tok_rows, HWIDE), PLANE)
    factor_back = exchange(factor_rows.reshape(SLICES, RANK, WIDTH), PLANE)

    gated_hidden_gradient = unpack(hidden_back)
    down_factor_grad = unpack(factor_back).T
    up_main = factor_back[:, :, 640:768].transpose(1, 0, 2).reshape(RANK, 4096)
    up_rest = factor_back[:, :, 576:592].transpose(1, 0, 2).reshape(RANK, 512)
    up_factor_grad = jnp.concatenate([up_main, up_rest], axis=1)

    router_logit_gradient, term = router_term(
        specialist_pairs, weights, gates, dispatcher_map, experts
    )
    attention_rows = kept.astype(F32) + passed.astype(F32)
    residual_input_gradient = (output_gradient.astype(jnp.float32) + term + attention_rows).astype(
        jnp.bfloat16
    )
    return (
        residual_input_gradient,
        gated_hidden_gradient,
        router_logit_gradient,
        down_factor_grad[None],
        up_factor_grad[None],
    )


def solution(mesh):
    fine = Mesh(mesh.devices.reshape(4, 2, 2, 4, 2), ("y", "xl", "xh", "z", "c"))
    rows2, rows3, heads = P(ROWS, None), P(ROWS, None, None), P(EP, TP)
    in_specs = (
        rows2,
        rows2,
        rows2,
        rows2,
        rows3,
        rows3,
        P(),
        heads,
        heads,
        heads,
        heads,
        P(None, TP),
        P(None, TP),
        P(None, TP),
        P(EP, None),
    )
    out_specs = (rows2, rows2, rows2, rows3, rows3)
    return jax.shard_map(local, mesh=fine, in_specs=in_specs, out_specs=out_specs, check_vma=False)
```

```python
import jax
import jax.numpy as jnp
from jax import lax
from jax.experimental import pallas as pl
from jax.experimental.pallas import tpu as pltpu
from jax.sharding import Mesh, PartitionSpec as P

HD = 128
RANK = 32
PLANE = ("xl", "xh", "z", "c")
LINE = "y"
TP = ("y", "xl")
EP = ("xh", "z", "c")
ROWS = ("xh", "z", "c", "y", "xl")

SLICES = 32
WIDTH = 768
HWIDE = 640
PAIRS = 16
GROUPS = 16
PAIR_ROWS = 48
SLOTS = GROUPS * PAIR_ROWS
GROUP_ROWS = PAIRS * PAIR_ROWS
STEP = 4
UNROLL = 4

adapter_scale = 2.0
score_cap = 50.0
query_scale = 144.0 ** (-0.5)
F32 = jnp.float32
BF16 = jnp.bfloat16
VMEM = 60 * 1024 * 1024


def attend_scores(queries, keys, lengths):
    rows = queries.shape[0]
    kv_count = keys.shape[1] // HD
    group = queries.shape[1] // keys.shape[1]
    query4 = queries.reshape(rows, kv_count, group, HD)
    key3 = keys.reshape(rows, kv_count, HD)
    places = jnp.arange(rows, dtype=jnp.int32)
    bounds = jnp.cumsum(lengths)
    docs = jnp.sum((places[:, None] >= bounds[None, :]).astype(jnp.int32), axis=1)
    allowed = (docs[:, None] == docs[None, :]) & (places[:, None] >= places[None, :])
    raw = (
        jnp.einsum("ikgd,jkd->kgij", query4, key3, preferred_element_type=jnp.float32) * query_scale
    )
    expo = jnp.where(allowed, jnp.exp(score_cap * jnp.tanh(raw / score_cap)), 0.0)
    return raw, jnp.sum(expo, axis=-1, keepdims=True), allowed


def attend_backward(
    raw,
    total,
    allowed,
    queries,
    keys,
    values,
    context_gradient,
    query_projection,
    key_projection,
    value_projection,
):
    rows = queries.shape[0]
    kv_count = keys.shape[1] // HD
    group = queries.shape[1] // keys.shape[1]
    query4 = queries.reshape(rows, kv_count, group, HD)
    ctx4 = context_gradient.reshape(rows, kv_count, group, HD)
    key3 = keys.reshape(rows, kv_count, HD)
    value3 = values.reshape(rows, kv_count, HD)
    bent = jnp.tanh(raw / score_cap)
    expo = jnp.where(allowed, jnp.exp(score_cap * bent), 0.0)
    probs = expo / total
    dprobs = jnp.einsum("ikgd,jkd->kgij", ctx4, value3, preferred_element_type=jnp.float32)
    dsoft = probs * (dprobs - jnp.sum(probs * dprobs, axis=-1, keepdims=True))
    dscore = (dsoft * (1.0 - bent * bent)).astype(jnp.bfloat16)
    probs_b = probs.astype(jnp.bfloat16)
    dquery = (
        (
            jnp.einsum("kgij,jkd->ikgd", dscore, key3, preferred_element_type=jnp.float32)
            * query_scale
        )
        .astype(jnp.bfloat16)
        .reshape(rows, -1)
    )
    dkey = (
        (
            jnp.einsum("kgij,ikgd->jkd", dscore, query4, preferred_element_type=jnp.float32)
            * query_scale
        )
        .astype(jnp.bfloat16)
        .reshape(rows, -1)
    )
    dvalue = (
        jnp.einsum("kgij,ikgd->jkd", probs_b, ctx4, preferred_element_type=jnp.float32)
        .astype(jnp.bfloat16)
        .reshape(rows, -1)
    )
    grads = jnp.concatenate([dquery, dkey, dvalue], axis=1)
    maps = jnp.concatenate([query_projection, key_projection, value_projection], axis=1)
    return jnp.einsum("te,de->td", grads, maps, preferred_element_type=jnp.float32)


def lanes_of(shape):
    return lax.broadcasted_iota(jnp.int32, shape, len(shape) - 1)


def pack_kernel(hm_ref, hr_ref, gm_ref, gr_ref, id_ref, out_ref):
    rows = hm_ref.shape[0]
    lane = lanes_of((rows, 128))
    ids = id_ref[...]
    for q in range(8):
        out_ref[q, :, 0:512] = hm_ref[:, 512 * q : 512 * q + 512]
        hid = hr_ref[:, 128 * (q // 2) : 128 * (q // 2) + 128].astype(F32)
        if q % 2:
            hid = pltpu.roll(hid, 64, 1)
        grad = pltpu.roll(gr_ref[...].astype(F32), (64 - 16 * q) % 128, 1)
        tail = jnp.where(lane < 64, hid, jnp.where(lane < 80, grad, ids))
        out_ref[q, :, 512:640] = tail.astype(BF16)
        out_ref[q, :, 640:768] = gm_ref[:, 128 * q : 128 * q + 128]


def pack(hid, grad, ids):
    rows = hid.shape[0]
    return pl.pallas_call(
        pack_kernel,
        grid=(4,),
        in_specs=[
            pl.BlockSpec((rows, 4096), lambda i: (0, i)),
            pl.BlockSpec((rows, 512), lambda i: (0, 32 + i)),
            pl.BlockSpec((rows, 1024), lambda i: (0, i)),
            pl.BlockSpec((rows, 128), lambda i: (0, 32 + i)),
            pl.BlockSpec((rows, 128), lambda i: (0, 0)),
        ],
        out_specs=pl.BlockSpec((8, rows, WIDTH), lambda i: (i, 0, 0)),
        out_shape=jax.ShapeDtypeStruct((SLICES, rows, WIDTH), BF16),
        compiler_params=pltpu.CompilerParams(vmem_limit_bytes=VMEM),
        cost_estimate=pl.CostEstimate(
            flops=rows * 2 * 24576, bytes_accessed=rows * 2 * 49152, transcendentals=0
        ),
        name="pack_slices",
    )(hid, hid, grad, grad, ids)


def unpack_kernel(main_ref, rem_ref, out_ref):
    step = pl.program_id(0)

    @pl.when(step < 4)
    def _():
        for q in range(8):
            out_ref[:, 512 * q : 512 * q + 512] = main_ref[q]

    @pl.when(step == 4)
    def _():
        lane = lanes_of(rem_ref.shape[1:])
        for d in range(16):
            low = rem_ref[2 * d].astype(F32)
            high = pltpu.roll(rem_ref[2 * d + 1].astype(F32), 64, 1)
            out_ref[:, 128 * d : 128 * d + 128] = jnp.where(lane < 64, low, high).astype(BF16)


def unpack(blocks):
    rows = blocks.shape[1]
    return pl.pallas_call(
        unpack_kernel,
        grid=(5,),
        in_specs=[
            pl.BlockSpec((8, rows, 512), lambda i: (jnp.minimum(i, 3), 0, 0)),
            pl.BlockSpec((SLICES, rows, 128), lambda i: (0, 0, 4), pipeline_mode=pl.Buffered(1)),
        ],
        out_specs=pl.BlockSpec((rows, 4096), lambda i: (0, i)),
        out_shape=jax.ShapeDtypeStruct((rows, 18432), BF16),
        compiler_params=pltpu.CompilerParams(vmem_limit_bytes=VMEM),
        cost_estimate=pl.CostEstimate(
            flops=rows * 18432, bytes_accessed=rows * 4 * 19000, transcendentals=0
        ),
        name="unpack_slices",
    )(blocks, blocks)


def hot(shape, axis, *slots):
    places = lax.broadcasted_iota(jnp.int32, shape, axis)
    found = places == slots[0]
    for s in slots[1:]:
        found = found | (places == s)
    return jnp.where(found, 1.0, 0.0).astype(BF16)


def slots_in_rows(tail):
    t = tail.astype(F32).T[80:88].astype(jnp.int32)
    second = jnp.where(lanes_of((1, 256)) >= 128, 3, 0)
    return [6 * t[k : k + 1] + t[2 + k : 3 + k] + second for k in range(2)]


def slots_in_columns(tail):
    t = tail.astype(F32)[:, 80:84].astype(jnp.int32)
    second = jnp.where(lax.broadcasted_iota(jnp.int32, (256, 1), 0) >= 128, 3, 0)
    return [6 * t[:, k : k + 1] + t[:, 2 + k : 3 + k] + second for k in range(2)]


def own_lanes(axis):
    shape = (GROUP_ROWS, 256) if axis == 0 else (256, GROUP_ROWS)
    slot = lax.broadcasted_iota(jnp.int32, shape, axis) % PAIR_ROWS // 6
    return slot == lax.broadcasted_iota(jnp.int32, shape, 1 - axis) // RANK


def repeat_lanes(k, axis):
    shape = (128, 256) if axis == 0 else (256, 128)
    a = lax.broadcasted_iota(jnp.int32, shape, axis)
    b = lax.broadcasted_iota(jnp.int32, shape, 1 - axis)
    return (a == b % RANK + RANK * k).astype(F32).astype(BF16)


def pair_at(q):
    return pl.ds(pl.multiple_of(q * 256, 256), 256)


def spread_pair(x):
    place = hot((SLOTS, 256), 0, *slots_in_rows(x[:, 512:640]))
    rows = jnp.dot(place, x, preferred_element_type=F32).astype(BF16)
    return rows.reshape(GROUPS, PAIR_ROWS, WIDTH)


def spread_kernel(x_ref, out_ref):
    for q in range(out_ref.shape[1]):
        out_ref[:, q] = spread_pair(x_ref[256 * q : 256 * q + 256])


def spread(x):
    return pl.pallas_call(
        spread_kernel,
        grid=(PAIRS // 2,),
        in_specs=[pl.BlockSpec((512, WIDTH), lambda i: (i, 0))],
        out_specs=pl.BlockSpec((GROUPS, 2, PAIR_ROWS, WIDTH), lambda i: (0, i, 0, 0)),
        out_shape=jax.ShapeDtypeStruct((GROUPS, PAIRS, PAIR_ROWS, WIDTH), BF16),
        compiler_params=pltpu.CompilerParams(vmem_limit_bytes=VMEM),
        cost_estimate=pl.CostEstimate(
            flops=2 * PAIRS * SLOTS * 256 * WIDTH,
            bytes_accessed=2 * PAIRS * (SLOTS + 256) * WIDTH,
            transcendentals=0,
        ),
        name="spread_rows",
    )(x)


def contract_kernel(x_ref, w_ref, out_ref, xs_ref, zs_ref):
    step = pl.program_id(0)

    @pl.when(step == 0)
    def _():
        def body(q, carry):
            xs_ref[:, q] = spread_pair(x_ref[pair_at(q)])
            return carry

        lax.fori_loop(0, PAIRS, body, 0, unroll=UNROLL)

    lane = lanes_of((256, 128))
    dims = (((1,), (1,)), ((), ()))
    mine = own_lanes(0)
    r = lax.broadcasted_iota(jnp.int32, (128, 128), 0) % RANK
    c = lax.broadcasted_iota(jnp.int32, (128, 128), 1)
    for n in range(STEP):
        group = step * STEP + n
        x = xs_ref[group].reshape(GROUP_ROWS, WIDTH)
        w = w_ref[256 * n : 256 * n + 256]
        tail = w[:, 512:640]
        zero = jnp.zeros_like(tail)
        w_h = jnp.concatenate([w[:, 0:512], jnp.where(lane < 64, tail, zero)], axis=1)
        w_g = jnp.concatenate([jnp.where(lane < 64, zero, tail), w[:, 640:768]], axis=1)
        out = jnp.zeros((GROUP_ROWS, 128), F32)
        for k, (w, cut) in enumerate(((w_h, slice(0, 640)), (w_g, slice(512, 768)))):
            full = lax.dot_general(x[:, cut], w, dims, preferred_element_type=F32)
            full = jnp.where(mine, full, 0.0)
            kept = (full[:, 0:128] + full[:, 128:256]).astype(BF16)
            fold = (c == r + RANK * k).astype(F32).astype(BF16)
            out += jnp.dot(kept, fold, preferred_element_type=F32)
        zs_ref[group] = out.astype(BF16).reshape(PAIRS, PAIR_ROWS, 128)

    @pl.when(step == GROUPS // STEP - 1)
    def _():
        half = lanes_of((256, 128))

        def body(q, carry):
            s0, s1 = slots_in_columns(x_ref[pair_at(q), 512:640])
            z = zs_ref[:, q].reshape(SLOTS, 128)
            place = hot((512, SLOTS), 1, jnp.concatenate([s0, s1], axis=0))
            found = jnp.dot(place, z, preferred_element_type=F32)
            out = jnp.where(half < 64, found[0:256], pltpu.roll(found[256:512], 64, 1))
            out_ref[pair_at(q)] = out.astype(BF16)
            return carry

        lax.fori_loop(0, PAIRS, body, 0, unroll=UNROLL)


def contract(x, w):
    return pl.pallas_call(
        contract_kernel,
        grid=(GROUPS // STEP,),
        in_specs=[
            pl.BlockSpec(x.shape, lambda i: (0, 0), pipeline_mode=pl.Buffered(1)),
            pl.BlockSpec((256 * STEP, WIDTH), lambda i: (i, 0)),
        ],
        out_specs=pl.BlockSpec((x.shape[0], 128), lambda i: (0, 0)),
        out_shape=jax.ShapeDtypeStruct((x.shape[0], 128), BF16),
        scratch_shapes=[
            pltpu.VMEM((GROUPS, PAIRS, PAIR_ROWS, WIDTH), BF16),
            pltpu.VMEM((GROUPS, PAIRS, PAIR_ROWS, 128), BF16),
        ],
        compiler_params=pltpu.CompilerParams(vmem_limit_bytes=VMEM),
        cost_estimate=pl.CostEstimate(
            flops=60 * GROUPS * GROUP_ROWS * 256 * 1024,
            bytes_accessed=4 * x.shape[0] * WIDTH,
            transcendentals=0,
        ),
        name="contract_experts",
    )(x, w)


def place_latents(t_ref, d_ref, ds_ref):
    half = lanes_of((256, 128))

    def body(q, carry):
        s0, s1 = slots_in_rows(t_ref[pair_at(q)])
        d = d_ref[pair_at(q)].astype(F32)
        d0 = jnp.where(half < 64, d, 0.0).astype(BF16)
        d1 = jnp.where(half < 64, pltpu.roll(d, 64, 1), 0.0).astype(BF16)
        place = hot((SLOTS, 512), 0, jnp.concatenate([s0, s1], axis=1))
        rows = jnp.dot(place, jnp.concatenate([d0, d1], axis=0), preferred_element_type=F32)
        ds_ref[:, q] = rows.astype(BF16).reshape(GROUPS, PAIR_ROWS, 128)
        return carry

    lax.fori_loop(0, PAIRS, body, 0, unroll=UNROLL)


def gradients_kernel(t_ref, d_ref, x_ref, w_ref, factor_ref, hidden_ref, ds_ref, gs_ref):
    step = pl.program_id(0)

    @pl.when(step == 0)
    def _():
        place_latents(t_ref, d_ref, ds_ref)

    dims = (((1,), (1,)), ((), ()))
    across, along = own_lanes(0), own_lanes(1)
    for n in range(STEP):
        group = step * STEP + n
        x = x_ref[n].reshape(GROUP_ROWS, WIDTH)
        d = ds_ref[group].reshape(GROUP_ROWS, 128)
        outs = []
        for k, cut in ((0, slice(0, 640)), (1, slice(512, 768))):
            wide = lax.dot_general(repeat_lanes(k, 1), d, dims, preferred_element_type=F32)
            wide = jnp.where(along, wide, 0.0).astype(BF16)
            outs.append(jnp.dot(wide, x[:, cut], preferred_element_type=F32))
        hid, grad = outs
        at = slice(256 * n, 256 * n + 256)
        factor_ref[at, 0:512] = hid[:, 0:512].astype(BF16)
        tail = jnp.where(lanes_of((256, 128)) < 64, hid[:, 512:640], grad[:, 0:128])
        factor_ref[at, 512:640] = tail.astype(BF16)
        factor_ref[at, 640:768] = grad[:, 128:256].astype(BF16)
        wide = jnp.dot(d, repeat_lanes(0, 0), preferred_element_type=F32)
        wide = jnp.where(across, wide, 0.0).astype(BF16)
        out = jnp.dot(wide, w_ref[at, 0:640], preferred_element_type=F32).astype(BF16)
        gs_ref[group] = out.reshape(PAIRS, PAIR_ROWS, HWIDE)

    @pl.when(step == GROUPS // STEP - 1)
    def _():
        def body(q, carry):
            both = hot((256, SLOTS), 1, *slots_in_columns(t_ref[pair_at(q)]))
            g = gs_ref[:, q].reshape(SLOTS, HWIDE)
            hidden_ref[pair_at(q)] = jnp.dot(both, g, preferred_element_type=F32).astype(BF16)
            return carry

        lax.fori_loop(0, PAIRS, body, 0, unroll=UNROLL)


def gradients(x, d, xs, w):
    rows = x.shape[0]
    once = pl.Buffered(1)
    return pl.pallas_call(
        gradients_kernel,
        grid=(GROUPS // STEP,),
        in_specs=[
            pl.BlockSpec((rows, 128), lambda i: (0, 4), pipeline_mode=once),
            pl.BlockSpec((rows, 128), lambda i: (0, 0), pipeline_mode=once),
            pl.BlockSpec((STEP, PAIRS, PAIR_ROWS, WIDTH), lambda i: (i, 0, 0, 0)),
            pl.BlockSpec((256 * STEP, WIDTH), lambda i: (i, 0)),
        ],
        out_specs=[
            pl.BlockSpec((256 * STEP, WIDTH), lambda i: (i, 0)),
            pl.BlockSpec((rows, HWIDE), lambda i: (0, 0), pipeline_mode=once),
        ],
        out_shape=[
            jax.ShapeDtypeStruct((GROUPS * 256, WIDTH), BF16),
            jax.ShapeDtypeStruct((rows, HWIDE), BF16),
        ],
        scratch_shapes=[
            pltpu.VMEM((GROUPS, PAIRS, PAIR_ROWS, 128), BF16),
            pltpu.VMEM((GROUPS, PAIRS, PAIR_ROWS, HWIDE), BF16),
        ],
        compiler_params=pltpu.CompilerParams(vmem_limit_bytes=VMEM),
        cost_estimate=pl.CostEstimate(
            flops=12 * GROUPS * GROUP_ROWS * 256 * 1024,
            bytes_accessed=2 * GROUPS * GROUP_ROWS * WIDTH + 8 * rows * WIDTH,
            transcendentals=0,
        ),
        name="factor_and_hidden_gradients",
    )(x, d, xs, w)


def router_term(specialist_pairs, weights, gates, dispatcher_map, experts):
    gate_val = gates.astype(jnp.float32)
    router_logit_gradient = weights * (
        gate_val - jnp.sum(weights * gate_val, axis=-1, keepdims=True)
    )
    ids = jnp.arange(experts, dtype=jnp.int32)
    expert_table = jnp.sum(
        jnp.where(
            specialist_pairs[:, :, None] == ids[None, None, :],
            router_logit_gradient[:, :, None],
            0.0,
        ),
        axis=1,
    )
    expert_table = expert_table.astype(jnp.bfloat16)
    term = jnp.einsum("te,de->td", expert_table, dispatcher_map, preferred_element_type=jnp.float32)
    return (router_logit_gradient, term)


def exchange(x, axes):
    return lax.all_to_all(x, axes, split_axis=0, concat_axis=0, tiled=True)


def local(
    hidden,
    output_gradient,
    specialist_pairs,
    chosen_router_logits,
    lowering_maps,
    raising_maps,
    dispatcher_map,
    queries,
    keys,
    values,
    context_gradient,
    query_projection,
    key_projection,
    value_projection,
    lengths,
):
    tok_rows = hidden.shape[0]
    width_d = output_gradient.shape[1]
    experts = 128
    tokens = tok_rows * SLICES
    place = specialist_pairs % 8 * 16 + specialist_pairs // 8
    lane = jnp.arange(128, dtype=jnp.int32)[None, :]
    named = (place[:, :, None] == lane[None]).astype(F32)
    earlier = jnp.tril(jnp.ones((tok_rows, tok_rows), BF16), -1)
    before = jnp.dot(earlier, jnp.sum(named, axis=1).astype(BF16), preferred_element_type=F32)
    rank = jnp.sum(named * before[:, None, :], axis=2)
    id_lanes = jnp.zeros((tok_rows, 128), F32)
    for at, column in enumerate((place[:, 0], place[:, 1], rank[:, 0], rank[:, 1])):
        id_lanes = jnp.where(lane == 80 + at, column.astype(F32)[:, None], id_lanes)
    w_mine = pack(lowering_maps[0].T, raising_maps[0], jnp.zeros((RANK, 128), F32))
    x_mine = pack(hidden, output_gradient, id_lanes)
    w_rows = exchange(w_mine, PLANE)
    scores = attend_scores(queries, keys, lengths[0])
    w_rows, x_mine, scores = lax.optimization_barrier((w_rows, x_mine, scores))
    w_all = lax.all_gather(w_rows.reshape(SLICES * RANK, WIDTH), LINE, axis=0, tiled=True)
    x = exchange(x_mine, PLANE).reshape(tokens, WIDTH)

    part = attend_backward(
        *scores,
        queries,
        keys,
        values,
        context_gradient,
        query_projection,
        key_projection,
        value_projection,
    ).astype(BF16)

    part_rows = lax.psum_scatter(part, LINE, scatter_dimension=0, tiled=True)
    x, _ = lax.optimization_barrier((x, part))
    sums = contract(x, w_all)
    x, sums = lax.optimization_barrier((x, sums))
    xs = spread(x)
    sums = exchange(sums.reshape(SLICES, tok_rows, 128), PLANE)
    xs, sums = lax.optimization_barrier((xs, sums))
    sums = jnp.sum(sums.astype(F32), axis=0)
    side = lax.axis_index("xl")
    halves = part_rows.reshape(2, tok_rows, width_d)
    kept = lax.dynamic_index_in_dim(halves, side, 0, keepdims=False)
    passed = lax.dynamic_index_in_dim(halves, 1 - side, 0, keepdims=False)
    passed = lax.ppermute(passed, "xl", [(0, 1), (1, 0)])

    weights = jax.nn.softmax(chosen_router_logits, axis=-1)
    weights_b = weights.astype(BF16).astype(F32)
    sent, gates = [], []
    for k in range(2):
        z = sums[:, 64 * k : 64 * k + 32].astype(BF16).astype(F32)
        p = sums[:, 64 * k + 32 : 64 * k + 64]
        w = weights_b[:, k : k + 1]
        gates.append(jnp.sum(adapter_scale * z * p, axis=-1, keepdims=True).astype(BF16))
        sent.append((adapter_scale * w * p).astype(BF16))
        sent.append(adapter_scale * (w * z).astype(BF16))
    mine = jnp.concatenate(sent, axis=1)
    d = exchange(jnp.broadcast_to(mine[None], (SLICES,) + mine.shape), PLANE)
    gates = jnp.concatenate(gates, axis=1)

    d = d.reshape(tokens, 128)
    factor_part, hidden_part = gradients(x, d, xs, w_all)
    factor_part, hidden_part, passed = lax.optimization_barrier(
        (factor_part, hidden_part, passed)
    )
    factor_rows = lax.psum_scatter(factor_part, LINE, scatter_dimension=0, tiled=True)
    hidden_back = exchange(hidden_part.reshape(SLICES, tok_rows, HWIDE), PLANE)
    factor_back = exchange(factor_rows.reshape(SLICES, RANK, WIDTH), PLANE)

    gated_hidden_gradient = unpack(hidden_back)
    down_factor_grad = unpack(factor_back).T
    up_main = factor_back[:, :, 640:768].transpose(1, 0, 2).reshape(RANK, 4096)
    up_rest = factor_back[:, :, 576:592].transpose(1, 0, 2).reshape(RANK, 512)
    up_factor_grad = jnp.concatenate([up_main, up_rest], axis=1)

    router_logit_gradient, term = router_term(
        specialist_pairs, weights, gates, dispatcher_map, experts
    )
    attention_rows = kept.astype(F32) + passed.astype(F32)
    residual_input_gradient = (output_gradient.astype(jnp.float32) + term + attention_rows).astype(
        jnp.bfloat16
    )
    return (
        residual_input_gradient,
        gated_hidden_gradient,
        router_logit_gradient,
        down_factor_grad[None],
        up_factor_grad[None],
    )


def solution(mesh):
    fine = Mesh(mesh.devices.reshape(4, 2, 2, 4, 2), ("y", "xl", "xh", "z", "c"))
    rows2, rows3, heads = P(ROWS, None), P(ROWS, None, None), P(EP, TP)
    in_specs = (
        rows2,
        rows2,
        rows2,
        rows2,
        rows3,
        rows3,
        P(),
        heads,
        heads,
        heads,
        heads,
        P(None, TP),
        P(None, TP),
        P(None, TP),
        P(EP, None),
    )
    out_specs = (rows2, rows2, rows2, rows3, rows3)
    return jax.shard_map(local, mesh=fine, in_specs=in_specs, out_specs=out_specs, check_vma=False)
```

```python
import jax
import jax.numpy as jnp
from jax import lax
from jax.experimental import pallas as pl
from jax.experimental.pallas import tpu as pltpu
from jax.sharding import Mesh, PartitionSpec as P

HD = 128
RANK = 32
PLANE = ("xl", "xh", "z", "c")
LINE = "y"
TP = ("y", "xl")
EP = ("xh", "z", "c")
ROWS = ("xh", "z", "c", "y", "xl")

SLICES = 32
WIDTH = 768
HWIDE = 640
PAIRS = 16
GROUPS = 16
PAIR_ROWS = 48
SLOTS = GROUPS * PAIR_ROWS
GROUP_ROWS = PAIRS * PAIR_ROWS
STEP = 4
UNROLL = 4

adapter_scale = 2.0
score_cap = 50.0
query_scale = 144.0 ** (-0.5)
F32 = jnp.float32
BF16 = jnp.bfloat16
VMEM = 60 * 1024 * 1024


def attend_scores(queries, keys, lengths):
    rows = queries.shape[0]
    kv_count = keys.shape[1] // HD
    group = queries.shape[1] // keys.shape[1]
    query4 = queries.reshape(rows, kv_count, group, HD)
    key3 = keys.reshape(rows, kv_count, HD)
    places = jnp.arange(rows, dtype=jnp.int32)
    bounds = jnp.cumsum(lengths)
    docs = jnp.sum((places[:, None] >= bounds[None, :]).astype(jnp.int32), axis=1)
    allowed = (docs[:, None] == docs[None, :]) & (places[:, None] >= places[None, :])
    raw = (
        jnp.einsum("ikgd,jkd->kgij", query4, key3, preferred_element_type=jnp.float32) * query_scale
    )
    expo = jnp.where(allowed, jnp.exp(score_cap * jnp.tanh(raw / score_cap)), 0.0)
    return raw, jnp.sum(expo, axis=-1, keepdims=True), allowed


def attend_backward(
    raw,
    total,
    allowed,
    queries,
    keys,
    values,
    context_gradient,
    query_projection,
    key_projection,
    value_projection,
):
    rows = queries.shape[0]
    kv_count = keys.shape[1] // HD
    group = queries.shape[1] // keys.shape[1]
    query4 = queries.reshape(rows, kv_count, group, HD)
    ctx4 = context_gradient.reshape(rows, kv_count, group, HD)
    key3 = keys.reshape(rows, kv_count, HD)
    value3 = values.reshape(rows, kv_count, HD)
    bent = jnp.tanh(raw / score_cap)
    expo = jnp.where(allowed, jnp.exp(score_cap * bent), 0.0)
    probs = expo / total
    dprobs = jnp.einsum("ikgd,jkd->kgij", ctx4, value3, preferred_element_type=jnp.float32)
    dsoft = probs * (dprobs - jnp.sum(probs * dprobs, axis=-1, keepdims=True))
    dscore = (dsoft * (1.0 - bent * bent)).astype(jnp.bfloat16)
    probs_b = probs.astype(jnp.bfloat16)
    dquery = (
        (
            jnp.einsum("kgij,jkd->ikgd", dscore, key3, preferred_element_type=jnp.float32)
            * query_scale
        )
        .astype(jnp.bfloat16)
        .reshape(rows, -1)
    )
    dkey = (
        (
            jnp.einsum("kgij,ikgd->jkd", dscore, query4, preferred_element_type=jnp.float32)
            * query_scale
        )
        .astype(jnp.bfloat16)
        .reshape(rows, -1)
    )
    dvalue = (
        jnp.einsum("kgij,ikgd->jkd", probs_b, ctx4, preferred_element_type=jnp.float32)
        .astype(jnp.bfloat16)
        .reshape(rows, -1)
    )
    grads = jnp.concatenate([dquery, dkey, dvalue], axis=1)
    maps = jnp.concatenate([query_projection, key_projection, value_projection], axis=1)
    return jnp.einsum("te,de->td", grads, maps, preferred_element_type=jnp.float32)


def lanes_of(shape):
    return lax.broadcasted_iota(jnp.int32, shape, len(shape) - 1)


def pack_kernel(hm_ref, hr_ref, gm_ref, gr_ref, id_ref, out_ref):
    rows = hm_ref.shape[0]
    lane = lanes_of((rows, 128))
    ids = id_ref[...]
    for q in range(8):
        out_ref[q, :, 0:512] = hm_ref[:, 512 * q : 512 * q + 512]
        hid = hr_ref[:, 128 * (q // 2) : 128 * (q // 2) + 128].astype(F32)
        if q % 2:
            hid = pltpu.roll(hid, 64, 1)
        grad = pltpu.roll(gr_ref[...].astype(F32), (64 - 16 * q) % 128, 1)
        tail = jnp.where(lane < 64, hid, jnp.where(lane < 80, grad, ids))
        out_ref[q, :, 512:640] = tail.astype(BF16)
        out_ref[q, :, 640:768] = gm_ref[:, 128 * q : 128 * q + 128]


def pack(hid, grad, ids):
    rows = hid.shape[0]
    return pl.pallas_call(
        pack_kernel,
        grid=(4,),
        in_specs=[
            pl.BlockSpec((rows, 4096), lambda i: (0, i)),
            pl.BlockSpec((rows, 512), lambda i: (0, 32 + i)),
            pl.BlockSpec((rows, 1024), lambda i: (0, i)),
            pl.BlockSpec((rows, 128), lambda i: (0, 32 + i)),
            pl.BlockSpec((rows, 128), lambda i: (0, 0)),
        ],
        out_specs=pl.BlockSpec((8, rows, WIDTH), lambda i: (i, 0, 0)),
        out_shape=jax.ShapeDtypeStruct((SLICES, rows, WIDTH), BF16),
        compiler_params=pltpu.CompilerParams(vmem_limit_bytes=VMEM),
        cost_estimate=pl.CostEstimate(
            flops=rows * 2 * 24576, bytes_accessed=rows * 2 * 49152, transcendentals=0
        ),
        name="pack_slices",
    )(hid, hid, grad, grad, ids)


def unpack_kernel(main_ref, rem_ref, out_ref):
    step = pl.program_id(0)

    @pl.when(step < 4)
    def _():
        for q in range(8):
            out_ref[:, 512 * q : 512 * q + 512] = main_ref[q]

    @pl.when(step == 4)
    def _():
        lane = lanes_of(rem_ref.shape[1:])
        for d in range(16):
            low = rem_ref[2 * d].astype(F32)
            high = pltpu.roll(rem_ref[2 * d + 1].astype(F32), 64, 1)
            out_ref[:, 128 * d : 128 * d + 128] = jnp.where(lane < 64, low, high).astype(BF16)


def unpack(blocks):
    rows = blocks.shape[1]
    return pl.pallas_call(
        unpack_kernel,
        grid=(5,),
        in_specs=[
            pl.BlockSpec((8, rows, 512), lambda i: (jnp.minimum(i, 3), 0, 0)),
            pl.BlockSpec((SLICES, rows, 128), lambda i: (0, 0, 4), pipeline_mode=pl.Buffered(1)),
        ],
        out_specs=pl.BlockSpec((rows, 4096), lambda i: (0, i)),
        out_shape=jax.ShapeDtypeStruct((rows, 18432), BF16),
        compiler_params=pltpu.CompilerParams(vmem_limit_bytes=VMEM),
        cost_estimate=pl.CostEstimate(
            flops=rows * 18432, bytes_accessed=rows * 4 * 19000, transcendentals=0
        ),
        name="unpack_slices",
    )(blocks, blocks)


def unpack_rows_kernel(main_ref, rem_ref, out_ref):
    step = pl.program_id(0)

    @pl.when(step < 8)
    def _():
        for q in range(4):
            out_ref[:, 512 * q : 512 * q + 512] = main_ref[q, 0:128]

    @pl.when(step == 8)
    def _():
        first = lanes_of((16, 128)) < 64
        for d in range(16):
            for b in range(8):
                tile = slice(128 * (b // 2), 128 * (b // 2) + 128)
                low = rem_ref[2 * d, :, tile].astype(F32)
                high = rem_ref[2 * d + 1, :, tile].astype(F32)
                if b % 2:
                    low = pltpu.roll(low, 64, 1)
                else:
                    high = pltpu.roll(high, 64, 1)
                both = jnp.where(first, low, high).astype(BF16)
                out_ref[16 * b : 16 * b + 16, 128 * d : 128 * d + 128] = both


def unpack_rows(blocks):
    return pl.pallas_call(
        unpack_rows_kernel,
        grid=(9,),
        in_specs=[
            pl.BlockSpec((4, 144, 512), lambda i: (jnp.minimum(i, 7), 0, 0)),
            pl.BlockSpec((SLICES, 16, 512), lambda i: (0, 8, 0), pipeline_mode=pl.Buffered(1)),
        ],
        out_specs=pl.BlockSpec((128, 2048), lambda i: (0, i)),
        out_shape=jax.ShapeDtypeStruct((128, 18432), BF16),
        compiler_params=pltpu.CompilerParams(vmem_limit_bytes=VMEM),
        cost_estimate=pl.CostEstimate(
            flops=128 * 18432, bytes_accessed=128 * 4 * 19000, transcendentals=0
        ),
        name="unpack_rows",
    )(blocks, blocks)


def hot(shape, axis, *slots):
    places = lax.broadcasted_iota(jnp.int32, shape, axis)
    found = places == slots[0]
    for s in slots[1:]:
        found = found | (places == s)
    return jnp.where(found, 1.0, 0.0).astype(BF16)


def slots_in_rows(tail):
    t = tail.astype(F32).T[80:88].astype(jnp.int32)
    second = jnp.where(lanes_of((1, 256)) >= 128, 3, 0)
    return [6 * t[k : k + 1] + t[2 + k : 3 + k] + second for k in range(2)]


def slots_in_columns(tail):
    t = tail.astype(F32)[:, 80:84].astype(jnp.int32)
    second = jnp.where(lax.broadcasted_iota(jnp.int32, (256, 1), 0) >= 128, 3, 0)
    return [6 * t[:, k : k + 1] + t[:, 2 + k : 3 + k] + second for k in range(2)]


def own_lanes(axis):
    shape = (GROUP_ROWS, 256) if axis == 0 else (256, GROUP_ROWS)
    slot = lax.broadcasted_iota(jnp.int32, shape, axis) % PAIR_ROWS // 6
    return slot == lax.broadcasted_iota(jnp.int32, shape, 1 - axis) // RANK


def repeat_lanes(k, axis):
    shape = (128, 256) if axis == 0 else (256, 128)
    a = lax.broadcasted_iota(jnp.int32, shape, axis)
    b = lax.broadcasted_iota(jnp.int32, shape, 1 - axis)
    return (a == b % RANK + RANK * k).astype(F32).astype(BF16)


def pair_at(q):
    return pl.ds(pl.multiple_of(q * 256, 256), 256)


def spread_pair(x):
    place = hot((SLOTS, 256), 0, *slots_in_rows(x[:, 512:640]))
    rows = jnp.dot(place, x, preferred_element_type=F32).astype(BF16)
    return rows.reshape(GROUPS, PAIR_ROWS, WIDTH)


def spread_kernel(x_ref, out_ref):
    for q in range(out_ref.shape[1]):
        out_ref[:, q] = spread_pair(x_ref[256 * q : 256 * q + 256])


def spread(x):
    return pl.pallas_call(
        spread_kernel,
        grid=(PAIRS // 2,),
        in_specs=[pl.BlockSpec((512, WIDTH), lambda i: (i, 0))],
        out_specs=pl.BlockSpec((GROUPS, 2, PAIR_ROWS, WIDTH), lambda i: (0, i, 0, 0)),
        out_shape=jax.ShapeDtypeStruct((GROUPS, PAIRS, PAIR_ROWS, WIDTH), BF16),
        compiler_params=pltpu.CompilerParams(vmem_limit_bytes=VMEM),
        cost_estimate=pl.CostEstimate(
            flops=2 * PAIRS * SLOTS * 256 * WIDTH,
            bytes_accessed=2 * PAIRS * (SLOTS + 256) * WIDTH,
            transcendentals=0,
        ),
        name="spread_rows",
    )(x)


def contract_kernel(x_ref, w_ref, out_ref, xs_ref, zs_ref):
    step = pl.program_id(0)

    @pl.when(step == 0)
    def _():
        def body(q, carry):
            xs_ref[:, q] = spread_pair(x_ref[pair_at(q)])
            return carry

        lax.fori_loop(0, PAIRS, body, 0, unroll=UNROLL)

    lane = lanes_of((256, 128))
    dims = (((1,), (1,)), ((), ()))
    mine = own_lanes(0)
    r = lax.broadcasted_iota(jnp.int32, (128, 128), 0) % RANK
    c = lax.broadcasted_iota(jnp.int32, (128, 128), 1)
    for n in range(STEP):
        group = step * STEP + n
        x = xs_ref[group].reshape(GROUP_ROWS, WIDTH)
        w = w_ref[256 * n : 256 * n + 256]
        tail = w[:, 512:640]
        zero = jnp.zeros_like(tail)
        w_h = jnp.concatenate([w[:, 0:512], jnp.where(lane < 64, tail, zero)], axis=1)
        w_g = jnp.concatenate([jnp.where(lane < 64, zero, tail), w[:, 640:768]], axis=1)
        out = jnp.zeros((GROUP_ROWS, 128), F32)
        for k, (w, cut) in enumerate(((w_h, slice(0, 640)), (w_g, slice(512, 768)))):
            full = lax.dot_general(x[:, cut], w, dims, preferred_element_type=F32)
            full = jnp.where(mine, full, 0.0)
            kept = (full[:, 0:128] + full[:, 128:256]).astype(BF16)
            fold = (c == r + RANK * k).astype(F32).astype(BF16)
            out += jnp.dot(kept, fold, preferred_element_type=F32)
        zs_ref[group] = out.astype(BF16).reshape(PAIRS, PAIR_ROWS, 128)

    @pl.when(step == GROUPS // STEP - 1)
    def _():
        half = lanes_of((256, 128))

        def body(q, carry):
            s0, s1 = slots_in_columns(x_ref[pair_at(q), 512:640])
            z = zs_ref[:, q].reshape(SLOTS, 128)
            place = hot((512, SLOTS), 1, jnp.concatenate([s0, s1], axis=0))
            found = jnp.dot(place, z, preferred_element_type=F32)
            out = jnp.where(half < 64, found[0:256], pltpu.roll(found[256:512], 64, 1))
            out_ref[pair_at(q)] = out.astype(BF16)
            return carry

        lax.fori_loop(0, PAIRS, body, 0, unroll=UNROLL)


def contract(x, w):
    return pl.pallas_call(
        contract_kernel,
        grid=(GROUPS // STEP,),
        in_specs=[
            pl.BlockSpec(x.shape, lambda i: (0, 0), pipeline_mode=pl.Buffered(1)),
            pl.BlockSpec((256 * STEP, WIDTH), lambda i: (i, 0)),
        ],
        out_specs=pl.BlockSpec((x.shape[0], 128), lambda i: (0, 0)),
        out_shape=jax.ShapeDtypeStruct((x.shape[0], 128), BF16),
        scratch_shapes=[
            pltpu.VMEM((GROUPS, PAIRS, PAIR_ROWS, WIDTH), BF16),
            pltpu.VMEM((GROUPS, PAIRS, PAIR_ROWS, 128), BF16),
        ],
        compiler_params=pltpu.CompilerParams(vmem_limit_bytes=VMEM),
        cost_estimate=pl.CostEstimate(
            flops=60 * GROUPS * GROUP_ROWS * 256 * 1024,
            bytes_accessed=4 * x.shape[0] * WIDTH,
            transcendentals=0,
        ),
        name="contract_experts",
    )(x, w)


def place_latents(t_ref, d_ref, ds_ref):
    half = lanes_of((256, 128))

    def body(q, carry):
        s0, s1 = slots_in_rows(t_ref[pair_at(q)])
        d = d_ref[pair_at(q)].astype(F32)
        d0 = jnp.where(half < 64, d, 0.0).astype(BF16)
        d1 = jnp.where(half < 64, pltpu.roll(d, 64, 1), 0.0).astype(BF16)
        place = hot((SLOTS, 512), 0, jnp.concatenate([s0, s1], axis=1))
        rows = jnp.dot(place, jnp.concatenate([d0, d1], axis=0), preferred_element_type=F32)
        ds_ref[:, q] = rows.astype(BF16).reshape(GROUPS, PAIR_ROWS, 128)
        return carry

    lax.fori_loop(0, PAIRS, body, 0, unroll=UNROLL)


def gradients_kernel(t_ref, d_ref, x_ref, w_ref, factor_ref, hidden_ref, ds_ref, gs_ref):
    step = pl.program_id(0)

    @pl.when(step == 0)
    def _():
        place_latents(t_ref, d_ref, ds_ref)

    dims = (((1,), (1,)), ((), ()))
    across, along = own_lanes(0), own_lanes(1)
    for n in range(STEP):
        group = step * STEP + n
        x = x_ref[n].reshape(GROUP_ROWS, WIDTH)
        d = ds_ref[group].reshape(GROUP_ROWS, 128)
        outs = []
        for k, cut in ((0, slice(0, 640)), (1, slice(512, 768))):
            wide = lax.dot_general(repeat_lanes(k, 1), d, dims, preferred_element_type=F32)
            wide = jnp.where(along, wide, 0.0).astype(BF16)
            outs.append(jnp.dot(wide, x[:, cut], preferred_element_type=F32))
        hid, grad = outs
        at = slice(256 * n, 256 * n + 256)
        factor_ref[at, 0:512] = hid[:, 0:512].astype(BF16)
        tail = jnp.where(lanes_of((256, 128)) < 64, hid[:, 512:640], grad[:, 0:128])
        factor_ref[at, 512:640] = tail.astype(BF16)
        factor_ref[at, 640:768] = grad[:, 128:256].astype(BF16)
        wide = jnp.dot(d, repeat_lanes(0, 0), preferred_element_type=F32)
        wide = jnp.where(across, wide, 0.0).astype(BF16)
        out = jnp.dot(wide, w_ref[at, 0:640], preferred_element_type=F32).astype(BF16)
        gs_ref[group] = out.reshape(PAIRS, PAIR_ROWS, HWIDE)

    @pl.when(step == GROUPS // STEP - 1)
    def _():
        def body(q, carry):
            both = hot((256, SLOTS), 1, *slots_in_columns(t_ref[pair_at(q)]))
            g = gs_ref[:, q].reshape(SLOTS, HWIDE)
            out = jnp.dot(both, g, preferred_element_type=F32)
            for h in range(2):
                block = out[128 * h : 128 * h + 128]
                hidden_ref[2 * q + h, 0:128] = block[:, 0:512].astype(BF16)
                for c in range(4):
                    low = block[32 * c : 32 * c + 16, 512:640]
                    high = pltpu.roll(block[32 * c + 16 : 32 * c + 32, 512:640], 64, 1)
                    both_halves = jnp.where(lanes_of((16, 128)) < 64, low, high).astype(BF16)
                    hidden_ref[2 * q + h, 128:144, 128 * c : 128 * c + 128] = both_halves
            return carry

        lax.fori_loop(0, PAIRS, body, 0, unroll=UNROLL)


def gradients(x, d, xs, w):
    rows = x.shape[0]
    once = pl.Buffered(1)
    return pl.pallas_call(
        gradients_kernel,
        grid=(GROUPS // STEP,),
        in_specs=[
            pl.BlockSpec((rows, 128), lambda i: (0, 4), pipeline_mode=once),
            pl.BlockSpec((rows, 128), lambda i: (0, 0), pipeline_mode=once),
            pl.BlockSpec((STEP, PAIRS, PAIR_ROWS, WIDTH), lambda i: (i, 0, 0, 0)),
            pl.BlockSpec((256 * STEP, WIDTH), lambda i: (i, 0)),
        ],
        out_specs=[
            pl.BlockSpec((256 * STEP, WIDTH), lambda i: (i, 0)),
            pl.BlockSpec((SLICES, 144, 512), lambda i: (0, 0, 0), pipeline_mode=once),
        ],
        out_shape=[
            jax.ShapeDtypeStruct((GROUPS * 256, WIDTH), BF16),
            jax.ShapeDtypeStruct((SLICES, 144, 512), BF16),
        ],
        scratch_shapes=[
            pltpu.VMEM((GROUPS, PAIRS, PAIR_ROWS, 128), BF16),
            pltpu.VMEM((GROUPS, PAIRS, PAIR_ROWS, HWIDE), BF16),
        ],
        compiler_params=pltpu.CompilerParams(vmem_limit_bytes=VMEM),
        cost_estimate=pl.CostEstimate(
            flops=12 * GROUPS * GROUP_ROWS * 256 * 1024,
            bytes_accessed=2 * GROUPS * GROUP_ROWS * WIDTH + 8 * rows * WIDTH,
            transcendentals=0,
        ),
        name="factor_and_hidden_gradients",
    )(x, d, xs, w)


def router_term(specialist_pairs, weights, gates, dispatcher_map, experts):
    gate_val = gates.astype(jnp.float32)
    router_logit_gradient = weights * (
        gate_val - jnp.sum(weights * gate_val, axis=-1, keepdims=True)
    )
    ids = jnp.arange(experts, dtype=jnp.int32)
    expert_table = jnp.sum(
        jnp.where(
            specialist_pairs[:, :, None] == ids[None, None, :],
            router_logit_gradient[:, :, None],
            0.0,
        ),
        axis=1,
    )
    expert_table = expert_table.astype(jnp.bfloat16)
    term = jnp.einsum("te,de->td", expert_table, dispatcher_map, preferred_element_type=jnp.float32)
    return (router_logit_gradient, term)


def exchange(x, axes):
    return lax.all_to_all(x, axes, split_axis=0, concat_axis=0, tiled=True)


def local(
    hidden,
    output_gradient,
    specialist_pairs,
    chosen_router_logits,
    lowering_maps,
    raising_maps,
    dispatcher_map,
    queries,
    keys,
    values,
    context_gradient,
    query_projection,
    key_projection,
    value_projection,
    lengths,
):
    tok_rows = hidden.shape[0]
    width_d = output_gradient.shape[1]
    experts = 128
    tokens = tok_rows * SLICES
    place = specialist_pairs % 8 * 16 + specialist_pairs // 8
    lane = jnp.arange(128, dtype=jnp.int32)[None, :]
    named = (place[:, :, None] == lane[None]).astype(F32)
    earlier = jnp.tril(jnp.ones((tok_rows, tok_rows), BF16), -1)
    before = jnp.dot(earlier, jnp.sum(named, axis=1).astype(BF16), preferred_element_type=F32)
    rank = jnp.sum(named * before[:, None, :], axis=2)
    id_lanes = jnp.zeros((tok_rows, 128), F32)
    for at, column in enumerate((place[:, 0], place[:, 1], rank[:, 0], rank[:, 1])):
        id_lanes = jnp.where(lane == 80 + at, column.astype(F32)[:, None], id_lanes)
    w_mine = pack(lowering_maps[0].T, raising_maps[0], jnp.zeros((RANK, 128), F32))
    x_mine = pack(hidden, output_gradient, id_lanes)
    w_rows = exchange(w_mine, PLANE)
    scores = attend_scores(queries, keys, lengths[0])
    w_rows, x_mine, scores = lax.optimization_barrier((w_rows, x_mine, scores))
    w_all = lax.all_gather(w_rows.reshape(SLICES * RANK, WIDTH), LINE, axis=0, tiled=True)
    x = exchange(x_mine, PLANE).reshape(tokens, WIDTH)

    part = attend_backward(
        *scores,
        queries,
        keys,
        values,
        context_gradient,
        query_projection,
        key_projection,
        value_projection,
    ).astype(BF16)

    part_rows = lax.psum_scatter(part, LINE, scatter_dimension=0, tiled=True)
    x, _ = lax.optimization_barrier((x, part))
    sums = contract(x, w_all)
    x, sums = lax.optimization_barrier((x, sums))
    xs = spread(x)
    sums = exchange(sums.reshape(SLICES, tok_rows, 128), PLANE)
    xs, sums = lax.optimization_barrier((xs, sums))
    sums = jnp.sum(sums.astype(F32), axis=0)
    side = lax.axis_index("xl")
    halves = part_rows.reshape(2, tok_rows, width_d)
    kept = lax.dynamic_index_in_dim(halves, side, 0, keepdims=False)
    passed = lax.dynamic_index_in_dim(halves, 1 - side, 0, keepdims=False)
    passed = lax.ppermute(passed, "xl", [(0, 1), (1, 0)])

    weights = jax.nn.softmax(chosen_router_logits, axis=-1)
    weights_b = weights.astype(BF16).astype(F32)
    sent, gates = [], []
    for k in range(2):
        z = sums[:, 64 * k : 64 * k + 32].astype(BF16).astype(F32)
        p = sums[:, 64 * k + 32 : 64 * k + 64]
        w = weights_b[:, k : k + 1]
        gates.append(jnp.sum(adapter_scale * z * p, axis=-1, keepdims=True).astype(BF16))
        sent.append((adapter_scale * w * p).astype(BF16))
        sent.append(adapter_scale * (w * z).astype(BF16))
    mine = jnp.concatenate(sent, axis=1)
    d = exchange(jnp.broadcast_to(mine[None], (SLICES,) + mine.shape), PLANE)
    gates = jnp.concatenate(gates, axis=1)

    d = d.reshape(tokens, 128)
    factor_part, hidden_part = gradients(x, d, xs, w_all)
    factor_part, hidden_part, passed = lax.optimization_barrier(
        (factor_part, hidden_part, passed)
    )
    factor_rows = lax.psum_scatter(factor_part, LINE, scatter_dimension=0, tiled=True)
    hidden_back = exchange(hidden_part, PLANE)
    factor_back = exchange(factor_rows.reshape(SLICES, RANK, WIDTH), PLANE)

    gated_hidden_gradient = unpack_rows(hidden_back)
    down_factor_grad = unpack(factor_back).T
    up_main = factor_back[:, :, 640:768].transpose(1, 0, 2).reshape(RANK, 4096)
    up_rest = factor_back[:, :, 576:592].transpose(1, 0, 2).reshape(RANK, 512)
    up_factor_grad = jnp.concatenate([up_main, up_rest], axis=1)

    router_logit_gradient, term = router_term(
        specialist_pairs, weights, gates, dispatcher_map, experts
    )
    attention_rows = kept.astype(F32) + passed.astype(F32)
    residual_input_gradient = (output_gradient.astype(jnp.float32) + term + attention_rows).astype(
        jnp.bfloat16
    )
    return (
        residual_input_gradient,
        gated_hidden_gradient,
        router_logit_gradient,
        down_factor_grad[None],
        up_factor_grad[None],
    )


def solution(mesh):
    fine = Mesh(mesh.devices.reshape(4, 2, 2, 4, 2), ("y", "xl", "xh", "z", "c"))
    rows2, rows3, heads = P(ROWS, None), P(ROWS, None, None), P(EP, TP)
    in_specs = (
        rows2,
        rows2,
        rows2,
        rows2,
        rows3,
        rows3,
        P(),
        heads,
        heads,
        heads,
        heads,
        P(None, TP),
        P(None, TP),
        P(None, TP),
        P(EP, None),
    )
    out_specs = (rows2, rows2, rows2, rows3, rows3)
    return jax.shard_map(local, mesh=fine, in_specs=in_specs, out_specs=out_specs, check_vma=False)
```

```python
import jax
import jax.numpy as jnp
from jax import lax
from jax.experimental import pallas as pl
from jax.experimental.pallas import tpu as pltpu
from jax.sharding import Mesh, PartitionSpec as P

HD = 128
RANK = 32
PLANE = ("xl", "xh", "z", "c")
LINE = "y"
TP = ("y", "xl")
EP = ("xh", "z", "c")
ROWS = ("xh", "z", "c", "y", "xl")

SLICES = 32
WIDTH = 768
HWIDE = 640
PAIRS = 16
GROUPS = 16
PAIR_ROWS = 48
SLOTS = GROUPS * PAIR_ROWS
GROUP_ROWS = PAIRS * PAIR_ROWS
STEP = 4
UNROLL = 8

adapter_scale = 2.0
score_cap = 50.0
query_scale = 144.0 ** (-0.5)
F32 = jnp.float32
BF16 = jnp.bfloat16
VMEM = 60 * 1024 * 1024


def attend_scores(queries, keys, lengths):
    rows = queries.shape[0]
    kv_count = keys.shape[1] // HD
    group = queries.shape[1] // keys.shape[1]
    query4 = queries.reshape(rows, kv_count, group, HD)
    key3 = keys.reshape(rows, kv_count, HD)
    places = jnp.arange(rows, dtype=jnp.int32)
    bounds = jnp.cumsum(lengths)
    docs = jnp.sum((places[:, None] >= bounds[None, :]).astype(jnp.int32), axis=1)
    allowed = (docs[:, None] == docs[None, :]) & (places[:, None] >= places[None, :])
    raw = (
        jnp.einsum("ikgd,jkd->kgij", query4, key3, preferred_element_type=jnp.float32) * query_scale
    )
    expo = jnp.where(allowed, jnp.exp(score_cap * jnp.tanh(raw / score_cap)), 0.0)
    return raw, jnp.sum(expo, axis=-1, keepdims=True), allowed


def attend_backward(
    raw,
    total,
    allowed,
    queries,
    keys,
    values,
    context_gradient,
    query_projection,
    key_projection,
    value_projection,
):
    rows = queries.shape[0]
    kv_count = keys.shape[1] // HD
    group = queries.shape[1] // keys.shape[1]
    query4 = queries.reshape(rows, kv_count, group, HD)
    ctx4 = context_gradient.reshape(rows, kv_count, group, HD)
    key3 = keys.reshape(rows, kv_count, HD)
    value3 = values.reshape(rows, kv_count, HD)
    bent = jnp.tanh(raw / score_cap)
    expo = jnp.where(allowed, jnp.exp(score_cap * bent), 0.0)
    probs = expo / total
    dprobs = jnp.einsum("ikgd,jkd->kgij", ctx4, value3, preferred_element_type=jnp.float32)
    dsoft = probs * (dprobs - jnp.sum(probs * dprobs, axis=-1, keepdims=True))
    dscore = (dsoft * (1.0 - bent * bent)).astype(jnp.bfloat16)
    probs_b = probs.astype(jnp.bfloat16)
    dquery = (
        (
            jnp.einsum("kgij,jkd->ikgd", dscore, key3, preferred_element_type=jnp.float32)
            * query_scale
        )
        .astype(jnp.bfloat16)
        .reshape(rows, -1)
    )
    dkey = (
        (
            jnp.einsum("kgij,ikgd->jkd", dscore, query4, preferred_element_type=jnp.float32)
            * query_scale
        )
        .astype(jnp.bfloat16)
        .reshape(rows, -1)
    )
    dvalue = (
        jnp.einsum("kgij,ikgd->jkd", probs_b, ctx4, preferred_element_type=jnp.float32)
        .astype(jnp.bfloat16)
        .reshape(rows, -1)
    )
    grads = jnp.concatenate([dquery, dkey, dvalue], axis=1)
    maps = jnp.concatenate([query_projection, key_projection, value_projection], axis=1)
    return jnp.einsum("te,de->td", grads, maps, preferred_element_type=jnp.float32)


def lanes_of(shape):
    return lax.broadcasted_iota(jnp.int32, shape, len(shape) - 1)


def pack_kernel(hm_ref, hr_ref, gm_ref, gr_ref, id_ref, out_ref):
    rows = hm_ref.shape[0]
    lane = lanes_of((rows, 128))
    ids = id_ref[...]
    for q in range(8):
        out_ref[q, :, 0:512] = hm_ref[:, 512 * q : 512 * q + 512]
        hid = hr_ref[:, 128 * (q // 2) : 128 * (q // 2) + 128].astype(F32)
        if q % 2:
            hid = pltpu.roll(hid, 64, 1)
        grad = pltpu.roll(gr_ref[...].astype(F32), (64 - 16 * q) % 128, 1)
        tail = jnp.where(lane < 64, hid, jnp.where(lane < 80, grad, ids))
        out_ref[q, :, 512:640] = tail.astype(BF16)
        out_ref[q, :, 640:768] = gm_ref[:, 128 * q : 128 * q + 128]


def pack(hid, grad, ids):
    rows = hid.shape[0]
    return pl.pallas_call(
        pack_kernel,
        grid=(4,),
        in_specs=[
            pl.BlockSpec((rows, 4096), lambda i: (0, i)),
            pl.BlockSpec((rows, 512), lambda i: (0, 32 + i)),
            pl.BlockSpec((rows, 1024), lambda i: (0, i)),
            pl.BlockSpec((rows, 128), lambda i: (0, 32 + i)),
            pl.BlockSpec((rows, 128), lambda i: (0, 0)),
        ],
        out_specs=pl.BlockSpec((8, rows, WIDTH), lambda i: (i, 0, 0)),
        out_shape=jax.ShapeDtypeStruct((SLICES, rows, WIDTH), BF16),
        compiler_params=pltpu.CompilerParams(vmem_limit_bytes=VMEM),
        cost_estimate=pl.CostEstimate(
            flops=rows * 2 * 24576, bytes_accessed=rows * 2 * 49152, transcendentals=0
        ),
        name="pack_slices",
    )(hid, hid, grad, grad, ids)


def unpack_kernel(main_ref, rem_ref, out_ref):
    step = pl.program_id(0)

    @pl.when(step < 4)
    def _():
        for q in range(8):
            out_ref[:, 512 * q : 512 * q + 512] = main_ref[q]

    @pl.when(step == 4)
    def _():
        lane = lanes_of(rem_ref.shape[1:])
        for d in range(16):
            low = rem_ref[2 * d].astype(F32)
            high = pltpu.roll(rem_ref[2 * d + 1].astype(F32), 64, 1)
            out_ref[:, 128 * d : 128 * d + 128] = jnp.where(lane < 64, low, high).astype(BF16)


def unpack(blocks):
    rows = blocks.shape[1]
    return pl.pallas_call(
        unpack_kernel,
        grid=(5,),
        in_specs=[
            pl.BlockSpec((8, rows, 512), lambda i: (jnp.minimum(i, 3), 0, 0)),
            pl.BlockSpec((SLICES, rows, 128), lambda i: (0, 0, 4), pipeline_mode=pl.Buffered(1)),
        ],
        out_specs=pl.BlockSpec((rows, 4096), lambda i: (0, i)),
        out_shape=jax.ShapeDtypeStruct((rows, 18432), BF16),
        compiler_params=pltpu.CompilerParams(vmem_limit_bytes=VMEM),
        cost_estimate=pl.CostEstimate(
            flops=rows * 18432, bytes_accessed=rows * 4 * 19000, transcendentals=0
        ),
        name="unpack_slices",
    )(blocks, blocks)


def unpack_rows_kernel(main_ref, rem_ref, out_ref):
    step = pl.program_id(0)

    @pl.when(step < 8)
    def _():
        for q in range(4):
            out_ref[:, 512 * q : 512 * q + 512] = main_ref[q, 0:128]

    @pl.when(step == 8)
    def _():
        first = lanes_of((16, 128)) < 64
        for d in range(16):
            for b in range(8):
                tile = slice(128 * (b // 2), 128 * (b // 2) + 128)
                low = rem_ref[2 * d, :, tile].astype(F32)
                high = rem_ref[2 * d + 1, :, tile].astype(F32)
                if b % 2:
                    low = pltpu.roll(low, 64, 1)
                else:
                    high = pltpu.roll(high, 64, 1)
                both = jnp.where(first, low, high).astype(BF16)
                out_ref[16 * b : 16 * b + 16, 128 * d : 128 * d + 128] = both


def unpack_rows(blocks):
    return pl.pallas_call(
        unpack_rows_kernel,
        grid=(9,),
        in_specs=[
            pl.BlockSpec((4, 144, 512), lambda i: (jnp.minimum(i, 7), 0, 0)),
            pl.BlockSpec((SLICES, 16, 512), lambda i: (0, 8, 0), pipeline_mode=pl.Buffered(1)),
        ],
        out_specs=pl.BlockSpec((128, 2048), lambda i: (0, i)),
        out_shape=jax.ShapeDtypeStruct((128, 18432), BF16),
        compiler_params=pltpu.CompilerParams(vmem_limit_bytes=VMEM),
        cost_estimate=pl.CostEstimate(
            flops=128 * 18432, bytes_accessed=128 * 4 * 19000, transcendentals=0
        ),
        name="unpack_rows",
    )(blocks, blocks)


def hot(shape, axis, *slots):
    places = lax.broadcasted_iota(jnp.int32, shape, axis)
    found = places == slots[0]
    for s in slots[1:]:
        found = found | (places == s)
    return jnp.where(found, 1.0, 0.0).astype(BF16)


def slots_in_rows(tail):
    t = tail.astype(F32).T[80:88].astype(jnp.int32)
    second = jnp.where(lanes_of((1, 256)) >= 128, 3, 0)
    return [6 * t[k : k + 1] + t[2 + k : 3 + k] + second for k in range(2)]


def slots_in_columns(tail):
    t = tail.astype(F32)[:, 80:84].astype(jnp.int32)
    second = jnp.where(lax.broadcasted_iota(jnp.int32, (256, 1), 0) >= 128, 3, 0)
    return [6 * t[:, k : k + 1] + t[:, 2 + k : 3 + k] + second for k in range(2)]


def own_lanes(axis):
    shape = (GROUP_ROWS, 256) if axis == 0 else (256, GROUP_ROWS)
    slot = lax.broadcasted_iota(jnp.int32, shape, axis) % PAIR_ROWS // 6
    return slot == lax.broadcasted_iota(jnp.int32, shape, 1 - axis) // RANK


def repeat_lanes(k, axis):
    shape = (128, 256) if axis == 0 else (256, 128)
    a = lax.broadcasted_iota(jnp.int32, shape, axis)
    b = lax.broadcasted_iota(jnp.int32, shape, 1 - axis)
    return (a == b % RANK + RANK * k).astype(F32).astype(BF16)


def pair_at(q):
    return pl.ds(pl.multiple_of(q * 256, 256), 256)


def spread_pair(x):
    place = hot((SLOTS, 256), 0, *slots_in_rows(x[:, 512:640]))
    rows = jnp.dot(place, x, preferred_element_type=F32).astype(BF16)
    return rows.reshape(GROUPS, PAIR_ROWS, WIDTH)


def spread_kernel(x_ref, out_ref):
    for q in range(out_ref.shape[1]):
        out_ref[:, q] = spread_pair(x_ref[256 * q : 256 * q + 256])


def spread(x):
    return pl.pallas_call(
        spread_kernel,
        grid=(PAIRS // 2,),
        in_specs=[pl.BlockSpec((512, WIDTH), lambda i: (i, 0))],
        out_specs=pl.BlockSpec((GROUPS, 2, PAIR_ROWS, WIDTH), lambda i: (0, i, 0, 0)),
        out_shape=jax.ShapeDtypeStruct((GROUPS, PAIRS, PAIR_ROWS, WIDTH), BF16),
        compiler_params=pltpu.CompilerParams(vmem_limit_bytes=VMEM),
        cost_estimate=pl.CostEstimate(
            flops=2 * PAIRS * SLOTS * 256 * WIDTH,
            bytes_accessed=2 * PAIRS * (SLOTS + 256) * WIDTH,
            transcendentals=0,
        ),
        name="spread_rows",
    )(x)


def contract_kernel(x_ref, w_ref, out_ref, xs_ref, zs_ref):
    step = pl.program_id(0)

    @pl.when(step == 0)
    def _():
        def body(q, carry):
            xs_ref[:, q] = spread_pair(x_ref[pair_at(q)])
            return carry

        lax.fori_loop(0, PAIRS, body, 0, unroll=UNROLL)

    lane = lanes_of((256, 128))
    dims = (((1,), (1,)), ((), ()))
    mine = own_lanes(0)
    r = lax.broadcasted_iota(jnp.int32, (128, 128), 0) % RANK
    c = lax.broadcasted_iota(jnp.int32, (128, 128), 1)
    for n in range(STEP):
        group = step * STEP + n
        x = xs_ref[group].reshape(GROUP_ROWS, WIDTH)
        w = w_ref[256 * n : 256 * n + 256]
        tail = w[:, 512:640]
        zero = jnp.zeros_like(tail)
        w_h = jnp.concatenate([w[:, 0:512], jnp.where(lane < 64, tail, zero)], axis=1)
        w_g = jnp.concatenate([jnp.where(lane < 64, zero, tail), w[:, 640:768]], axis=1)
        out = jnp.zeros((GROUP_ROWS, 128), F32)
        for k, (w, cut) in enumerate(((w_h, slice(0, 640)), (w_g, slice(512, 768)))):
            full = lax.dot_general(x[:, cut], w, dims, preferred_element_type=F32)
            full = jnp.where(mine, full, 0.0)
            kept = (full[:, 0:128] + full[:, 128:256]).astype(BF16)
            fold = (c == r + RANK * k).astype(F32).astype(BF16)
            out += jnp.dot(kept, fold, preferred_element_type=F32)
        zs_ref[group] = out.astype(BF16).reshape(PAIRS, PAIR_ROWS, 128)

    @pl.when(step == GROUPS // STEP - 1)
    def _():
        half = lanes_of((256, 128))

        def body(q, carry):
            s0, s1 = slots_in_columns(x_ref[pair_at(q), 512:640])
            z = zs_ref[:, q].reshape(SLOTS, 128)
            place = hot((512, SLOTS), 1, jnp.concatenate([s0, s1], axis=0))
            found = jnp.dot(place, z, preferred_element_type=F32)
            out = jnp.where(half < 64, found[0:256], pltpu.roll(found[256:512], 64, 1))
            out_ref[pair_at(q)] = out.astype(BF16)
            return carry

        lax.fori_loop(0, PAIRS, body, 0, unroll=UNROLL)


def contract(x, w):
    return pl.pallas_call(
        contract_kernel,
        grid=(GROUPS // STEP,),
        in_specs=[
            pl.BlockSpec(x.shape, lambda i: (0, 0), pipeline_mode=pl.Buffered(1)),
            pl.BlockSpec((256 * STEP, WIDTH), lambda i: (i, 0)),
        ],
        out_specs=pl.BlockSpec((x.shape[0], 128), lambda i: (0, 0)),
        out_shape=jax.ShapeDtypeStruct((x.shape[0], 128), BF16),
        scratch_shapes=[
            pltpu.VMEM((GROUPS, PAIRS, PAIR_ROWS, WIDTH), BF16),
            pltpu.VMEM((GROUPS, PAIRS, PAIR_ROWS, 128), BF16),
        ],
        compiler_params=pltpu.CompilerParams(vmem_limit_bytes=VMEM),
        cost_estimate=pl.CostEstimate(
            flops=60 * GROUPS * GROUP_ROWS * 256 * 1024,
            bytes_accessed=4 * x.shape[0] * WIDTH,
            transcendentals=0,
        ),
        name="contract_experts",
    )(x, w)


def place_latents(t_ref, d_ref, ds_ref):
    half = lanes_of((256, 128))

    def body(q, carry):
        s0, s1 = slots_in_rows(t_ref[pair_at(q)])
        d = d_ref[pair_at(q)].astype(F32)
        d0 = jnp.where(half < 64, d, 0.0).astype(BF16)
        d1 = jnp.where(half < 64, pltpu.roll(d, 64, 1), 0.0).astype(BF16)
        place = hot((SLOTS, 512), 0, jnp.concatenate([s0, s1], axis=1))
        rows = jnp.dot(place, jnp.concatenate([d0, d1], axis=0), preferred_element_type=F32)
        ds_ref[:, q] = rows.astype(BF16).reshape(GROUPS, PAIR_ROWS, 128)
        return carry

    lax.fori_loop(0, PAIRS, body, 0, unroll=UNROLL)


def gradients_kernel(t_ref, d_ref, x_ref, w_ref, factor_ref, hidden_ref, ds_ref, gs_ref):
    step = pl.program_id(0)

    @pl.when(step == 0)
    def _():
        place_latents(t_ref, d_ref, ds_ref)

    dims = (((1,), (1,)), ((), ()))
    across, along = own_lanes(0), own_lanes(1)
    for n in range(STEP):
        group = step * STEP + n
        x = x_ref[n].reshape(GROUP_ROWS, WIDTH)
        d = ds_ref[group].reshape(GROUP_ROWS, 128)
        outs = []
        for k, cut in ((0, slice(0, 640)), (1, slice(512, 768))):
            wide = lax.dot_general(repeat_lanes(k, 1), d, dims, preferred_element_type=F32)
            wide = jnp.where(along, wide, 0.0).astype(BF16)
            outs.append(jnp.dot(wide, x[:, cut], preferred_element_type=F32))
        hid, grad = outs
        at = slice(256 * n, 256 * n + 256)
        factor_ref[at, 0:512] = hid[:, 0:512].astype(BF16)
        tail = jnp.where(lanes_of((256, 128)) < 64, hid[:, 512:640], grad[:, 0:128])
        factor_ref[at, 512:640] = tail.astype(BF16)
        factor_ref[at, 640:768] = grad[:, 128:256].astype(BF16)
        wide = jnp.dot(d, repeat_lanes(0, 0), preferred_element_type=F32)
        wide = jnp.where(across, wide, 0.0).astype(BF16)
        out = jnp.dot(wide, w_ref[at, 0:640], preferred_element_type=F32).astype(BF16)
        gs_ref[group] = out.reshape(PAIRS, PAIR_ROWS, HWIDE)

    @pl.when(step == GROUPS // STEP - 1)
    def _():
        def body(q, carry):
            both = hot((256, SLOTS), 1, *slots_in_columns(t_ref[pair_at(q)]))
            g = gs_ref[:, q].reshape(SLOTS, HWIDE)
            out = jnp.dot(both, g, preferred_element_type=F32)
            for h in range(2):
                block = out[128 * h : 128 * h + 128]
                hidden_ref[2 * q + h, 0:128] = block[:, 0:512].astype(BF16)
                for c in range(4):
                    low = block[32 * c : 32 * c + 16, 512:640]
                    high = pltpu.roll(block[32 * c + 16 : 32 * c + 32, 512:640], 64, 1)
                    both_halves = jnp.where(lanes_of((16, 128)) < 64, low, high).astype(BF16)
                    hidden_ref[2 * q + h, 128:144, 128 * c : 128 * c + 128] = both_halves
            return carry

        lax.fori_loop(0, PAIRS, body, 0, unroll=UNROLL)


def gradients(x, d, xs, w):
    rows = x.shape[0]
    once = pl.Buffered(1)
    return pl.pallas_call(
        gradients_kernel,
        grid=(GROUPS // STEP,),
        in_specs=[
            pl.BlockSpec((rows, 128), lambda i: (0, 4), pipeline_mode=once),
            pl.BlockSpec((rows, 128), lambda i: (0, 0), pipeline_mode=once),
            pl.BlockSpec((STEP, PAIRS, PAIR_ROWS, WIDTH), lambda i: (i, 0, 0, 0)),
            pl.BlockSpec((256 * STEP, WIDTH), lambda i: (i, 0)),
        ],
        out_specs=[
            pl.BlockSpec((256 * STEP, WIDTH), lambda i: (i, 0)),
            pl.BlockSpec((SLICES, 144, 512), lambda i: (0, 0, 0), pipeline_mode=once),
        ],
        out_shape=[
            jax.ShapeDtypeStruct((GROUPS * 256, WIDTH), BF16),
            jax.ShapeDtypeStruct((SLICES, 144, 512), BF16),
        ],
        scratch_shapes=[
            pltpu.VMEM((GROUPS, PAIRS, PAIR_ROWS, 128), BF16),
            pltpu.VMEM((GROUPS, PAIRS, PAIR_ROWS, HWIDE), BF16),
        ],
        compiler_params=pltpu.CompilerParams(vmem_limit_bytes=VMEM),
        cost_estimate=pl.CostEstimate(
            flops=12 * GROUPS * GROUP_ROWS * 256 * 1024,
            bytes_accessed=2 * GROUPS * GROUP_ROWS * WIDTH + 8 * rows * WIDTH,
            transcendentals=0,
        ),
        name="factor_and_hidden_gradients",
    )(x, d, xs, w)


def router_term(specialist_pairs, weights, gates, dispatcher_map, experts):
    gate_val = gates.astype(jnp.float32)
    router_logit_gradient = weights * (
        gate_val - jnp.sum(weights * gate_val, axis=-1, keepdims=True)
    )
    ids = jnp.arange(experts, dtype=jnp.int32)
    expert_table = jnp.sum(
        jnp.where(
            specialist_pairs[:, :, None] == ids[None, None, :],
            router_logit_gradient[:, :, None],
            0.0,
        ),
        axis=1,
    )
    expert_table = expert_table.astype(jnp.bfloat16)
    term = jnp.einsum("te,de->td", expert_table, dispatcher_map, preferred_element_type=jnp.float32)
    return (router_logit_gradient, term)


def exchange(x, axes):
    return lax.all_to_all(x, axes, split_axis=0, concat_axis=0, tiled=True)


def local(
    hidden,
    output_gradient,
    specialist_pairs,
    chosen_router_logits,
    lowering_maps,
    raising_maps,
    dispatcher_map,
    queries,
    keys,
    values,
    context_gradient,
    query_projection,
    key_projection,
    value_projection,
    lengths,
):
    tok_rows = hidden.shape[0]
    width_d = output_gradient.shape[1]
    experts = 128
    tokens = tok_rows * SLICES
    place = specialist_pairs % 8 * 16 + specialist_pairs // 8
    lane = jnp.arange(128, dtype=jnp.int32)[None, :]
    named = (place[:, :, None] == lane[None]).astype(F32)
    earlier = jnp.tril(jnp.ones((tok_rows, tok_rows), BF16), -1)
    before = jnp.dot(earlier, jnp.sum(named, axis=1).astype(BF16), preferred_element_type=F32)
    rank = jnp.sum(named * before[:, None, :], axis=2)
    id_lanes = jnp.zeros((tok_rows, 128), F32)
    for at, column in enumerate((place[:, 0], place[:, 1], rank[:, 0], rank[:, 1])):
        id_lanes = jnp.where(lane == 80 + at, column.astype(F32)[:, None], id_lanes)
    w_mine = pack(lowering_maps[0].T, raising_maps[0], jnp.zeros((RANK, 128), F32))
    x_mine = pack(hidden, output_gradient, id_lanes)
    w_rows = exchange(w_mine, PLANE)
    scores = attend_scores(queries, keys, lengths[0])
    w_rows, x_mine, scores = lax.optimization_barrier((w_rows, x_mine, scores))
    w_all = lax.all_gather(w_rows.reshape(SLICES * RANK, WIDTH), LINE, axis=0, tiled=True)
    x = exchange(x_mine, PLANE).reshape(tokens, WIDTH)

    part = attend_backward(
        *scores,
        queries,
        keys,
        values,
        context_gradient,
        query_projection,
        key_projection,
        value_projection,
    ).astype(BF16)

    part_rows = lax.psum_scatter(part, LINE, scatter_dimension=0, tiled=True)
    x, _ = lax.optimization_barrier((x, part))
    sums = contract(x, w_all)
    x, sums = lax.optimization_barrier((x, sums))
    xs = spread(x)
    sums = exchange(sums.reshape(SLICES, tok_rows, 128), PLANE)
    xs, sums = lax.optimization_barrier((xs, sums))
    sums = jnp.sum(sums.astype(F32), axis=0)
    side = lax.axis_index("xl")
    halves = part_rows.reshape(2, tok_rows, width_d)
    kept = lax.dynamic_index_in_dim(halves, side, 0, keepdims=False)
    passed = lax.dynamic_index_in_dim(halves, 1 - side, 0, keepdims=False)
    passed = lax.ppermute(passed, "xl", [(0, 1), (1, 0)])

    weights = jax.nn.softmax(chosen_router_logits, axis=-1)
    weights_b = weights.astype(BF16).astype(F32)
    sent, gates = [], []
    for k in range(2):
        z = sums[:, 64 * k : 64 * k + 32].astype(BF16).astype(F32)
        p = sums[:, 64 * k + 32 : 64 * k + 64]
        w = weights_b[:, k : k + 1]
        gates.append(jnp.sum(adapter_scale * z * p, axis=-1, keepdims=True).astype(BF16))
        sent.append((adapter_scale * w * p).astype(BF16))
        sent.append(adapter_scale * (w * z).astype(BF16))
    mine = jnp.concatenate(sent, axis=1)
    d = exchange(jnp.broadcast_to(mine[None], (SLICES,) + mine.shape), PLANE)
    gates = jnp.concatenate(gates, axis=1)

    d = d.reshape(tokens, 128)
    factor_part, hidden_part = gradients(x, d, xs, w_all)
    factor_part, hidden_part, passed = lax.optimization_barrier(
        (factor_part, hidden_part, passed)
    )
    factor_rows = lax.psum_scatter(factor_part, LINE, scatter_dimension=0, tiled=True)
    hidden_back = exchange(hidden_part, PLANE)
    factor_back = exchange(factor_rows.reshape(SLICES, RANK, WIDTH), PLANE)

    gated_hidden_gradient = unpack_rows(hidden_back)
    down_factor_grad = unpack(factor_back).T
    up_main = factor_back[:, :, 640:768].transpose(1, 0, 2).reshape(RANK, 4096)
    up_rest = factor_back[:, :, 576:592].transpose(1, 0, 2).reshape(RANK, 512)
    up_factor_grad = jnp.concatenate([up_main, up_rest], axis=1)

    router_logit_gradient, term = router_term(
        specialist_pairs, weights, gates, dispatcher_map, experts
    )
    attention_rows = kept.astype(F32) + passed.astype(F32)
    residual_input_gradient = (output_gradient.astype(jnp.float32) + term + attention_rows).astype(
        jnp.bfloat16
    )
    return (
        residual_input_gradient,
        gated_hidden_gradient,
        router_logit_gradient,
        down_factor_grad[None],
        up_factor_grad[None],
    )


def solution(mesh):
    fine = Mesh(mesh.devices.reshape(4, 2, 2, 4, 2), ("y", "xl", "xh", "z", "c"))
    rows2, rows3, heads = P(ROWS, None), P(ROWS, None, None), P(EP, TP)
    in_specs = (
        rows2,
        rows2,
        rows2,
        rows2,
        rows3,
        rows3,
        P(),
        heads,
        heads,
        heads,
        heads,
        P(None, TP),
        P(None, TP),
        P(None, TP),
        P(EP, None),
    )
    out_specs = (rows2, rows2, rows2, rows3, rows3)
    return jax.shard_map(local, mesh=fine, in_specs=in_specs, out_specs=out_specs, check_vma=False)
```
